128 devices in a mesh: aa: 8 (over z, core), ba: 16 (over x, y).
Axes of the slice: x: 4, y: 4, z: 4, core: 2. Of those that a mesh axis runs over, the one named last changes fastest.
Arguments:
- points_a: float32 [8192, 256], P(('aa', 'ba')), may hold values from -20 to 20, as said below
- points_b: float32 [65536, 256], P(('ba', 'aa')), may hold values from -20 to 20, as said below
Outputs:
- potential_a: float32 [8192], P('aa')
- potential_b: float32 [65536], P('ba')
- grad_a: float32 [8192, 256], P(('aa', 'ba'))
The draws below stay inside these ranges and needn't reach their ends.
Inputs may be any that keep to these rules, and one draw needn't show every extreme that they name: `points_a`: Real-valued embeddings whose entries stay within the range. `points_b`: Real-valued embeddings whose entries stay within the range.
All inputs are finite; a program needn't handle non-finite values.
Results may differ from the reference program's by a relative error of at most 0.0003.
Values sent between devices are 32-bit elements; how exact they have to be, the bound alone decides.
No kernel may reach another device: no remote copies, remote signals or barrier semaphores. Data moves between devices by JAX's collectives and lax.ppermute only.
A program may use at most 64 MiB of HBM per device.

```python
import jax
import jax.numpy as jnp
from jax import lax

W = 256
ITERS = 2
N = 8192
M = 65536


def shared_points(key, scale_lo, scale_hi):
    keys = jax.random.split(key, 4)
    base_a = jnp.clip(jax.random.normal(keys[0], (N, W), jnp.float32), -5.0, 5.0)
    base_b = jnp.clip(jax.random.normal(keys[1], (M, W), jnp.float32), -5.0, 5.0)
    log_lo = jnp.log(jnp.float32(scale_lo))
    log_hi = jnp.log(jnp.float32(scale_hi))
    scale_a = jnp.exp(jax.random.uniform(keys[2], (N, 1), jnp.float32, log_lo, log_hi))
    scale_b = jnp.exp(jax.random.uniform(keys[3], (M, 1), jnp.float32, log_lo, log_hi))
    base_a = base_a * scale_a
    base_b = base_b * scale_b
    base_a = base_a.at[0:8].set(base_a[0:8])
    base_b = base_b.at[8:16].set(base_b[8:16])
    base_a = jnp.clip(base_a, -20.0, 20.0)
    base_b = jnp.clip(base_b, -20.0, 20.0)
    return (base_a, base_b)


def draw_points_a(key, part):
    pair = shared_points(key, 0.8, 1.25)
    return pair[0]


def draw_points_b(key, part):
    pair = shared_points(key, 0.8, 1.25)
    return pair[1]


def setup_inputs(seed: int = 0) -> dict:
    seeds = jax.random.split(jax.random.key(seed), 3)
    return {
        "points_a": draw_points_a(jax.random.fold_in(seeds[2], 71), 0),
        "points_b": draw_points_b(jax.random.fold_in(seeds[2], 71), 0),
    }


HIGH = lax.Precision.HIGHEST


def cost_tile(rows, row_norms, cols, col_norms):
    cross = jnp.einsum("iw,jw->ij", rows, cols, precision=HIGH, preferred_element_type=jnp.float32)
    return row_norms[:, None] + col_norms[None, :] - 2.0 * cross


def combine_pairs(first, second):
    peak = jnp.maximum(first[0], second[0])
    total = first[1] * jnp.exp(first[0] - peak) + second[1] * jnp.exp(second[0] - peak)
    return (peak, total)


def reference(points_a, points_b):
    count_a, width = points_a.shape
    count_b = points_b.shape[0]
    eps = width / 8.0
    log_a = -jnp.log(jnp.float32(count_a))
    log_b = -jnp.log(jnp.float32(count_b))
    norms_a = jnp.sum(points_a * points_a, axis=1)
    norms_b = jnp.sum(points_b * points_b, axis=1)
    block = min(512, count_a)
    number = count_a // block
    blocks_a = points_a.reshape(number, block, width)
    bnorms_a = norms_a.reshape(number, block)

    def row_update(pot_b):
        def one_block(item):
            xs, ns = item
            scores = (pot_b[None, :] - cost_tile(xs, ns, points_b, norms_b)) / eps + log_b
            return -eps * jax.nn.logsumexp(scores, axis=1)
        return lax.map(one_block, (blocks_a, bnorms_a)).reshape(count_a)

    def col_update(pot_a):
        blocks_f = pot_a.reshape(number, block)

        def step(carry, item):
            xs, ns, fs = item
            scores = (fs[:, None] - cost_tile(xs, ns, points_b, norms_b)) / eps + log_a
            peak = jnp.max(scores, axis=0)
            total = jnp.sum(jnp.exp(scores - peak[None, :]), axis=0)
            return combine_pairs(carry, (peak, total)), None

        init = (jnp.full((count_b,), -1e30, jnp.float32), jnp.zeros((count_b,), jnp.float32))
        (peak, total), unused = lax.scan(step, init, (blocks_a, bnorms_a, blocks_f))
        return -eps * (peak + jnp.log(total))

    pot_b = jnp.zeros((count_b,), jnp.float32)
    pot_a = jnp.zeros((count_a,), jnp.float32)
    for turn in range(ITERS):
        pot_a = row_update(pot_b)
        pot_b = col_update(pot_a)

    def grad_block(item):
        xs, ns, fs = item
        tile_q = jnp.exp((fs[:, None] + pot_b[None, :] - cost_tile(xs, ns, points_b, norms_b)) / eps + log_b)
        mass = jnp.sum(tile_q, axis=1)
        pulled = jnp.dot(tile_q, points_b, precision=HIGH, preferred_element_type=jnp.float32)
        return 2.0 * (xs * mass[:, None] - pulled)

    grad_a = lax.map(grad_block, (blocks_a, bnorms_a, pot_a.reshape(number, block))).reshape(count_a, width)
    return (pot_a, pot_b, grad_a)
```

```python
import math

import jax
import jax.numpy as jnp
from jax import lax
from jax.experimental import pallas as pl
from jax.experimental.pallas import tpu as pltpu
from jax.sharding import PartitionSpec as P

ITERS = 2
LOG2E = math.log2(math.e)
LANES = 128
MIB = 1024 * 1024


def split(x):
    hi = x.astype(jnp.bfloat16)
    return hi, (x - hi.astype(jnp.float32)).astype(jnp.bfloat16)


def row_norms(x):
    sq = x * x
    part = sq[:, :LANES]
    for k in range(LANES, sq.shape[1], LANES):
        part = part + sq[:, k:k + LANES]
    return jnp.sum(part.T, axis=0, keepdims=True)


def combine(parts):
    top = jnp.max(parts, axis=0, keepdims=True)
    return top + jnp.log2(jnp.sum(jnp.exp2(parts - top), axis=0, keepdims=True))


def scores_kernel(eps, places, a_ref, *refs):
    pieces, (s_ref, bhi_ref, blo_ref, a2_ref, b2_ref, left) = refs[:len(places)], refs[len(places):]
    x = a_ref[...]
    a2_ref[...] = row_norms(x) * (LOG2E / eps)
    hi, lo = split(x * (2.0 * LOG2E / eps))
    left[...] = jnp.concatenate([hi, hi, lo], axis=1)
    me = lax.axis_index("aa")
    dims = (((1,), (1,)), ((), ()))
    for ref, place in zip(pieces, places):
        rows = ref.shape[0]
        at = pl.ds(pl.multiple_of(place(me), rows), rows)
        y = ref[...]
        b2_ref[:, at] = row_norms(y) * (LOG2E / eps)
        hi, lo = split(y)
        bhi_ref[at, :] = hi
        blo_ref[at, :] = lo
        right = jnp.concatenate([hi, lo, hi], axis=1)
        s_ref[:, at] = lax.dot_general(left[...], right, dims, preferred_element_type=jnp.float32)


def row_pass_kernel(log_a, first, part_ref, b2_ref, s_ref, out_ref, beta_ref, wide, top, tot):
    beta = -b2_ref[...] if first else -combine(part_ref[...]) - log_a
    beta_ref[...] = beta
    wide[...] = jnp.broadcast_to(beta, wide.shape)
    cols = s_ref.shape[1] // LANES

    def group(r, carry):
        rows = pl.ds(pl.multiple_of(r * 8, 8), 8)
        x = [s_ref[rows, k * LANES:(k + 1) * LANES] + wide[:, k * LANES:(k + 1) * LANES] for k in range(cols)]
        m = tree(jnp.maximum, x)
        top[rows, :] = m
        tot[rows, :] = tree(jnp.add, [jnp.exp2(v - m) for v in x])
        return carry

    lax.fori_loop(0, s_ref.shape[0] // 8, group, 0, unroll=2)
    m = top[...].T
    peak = jnp.max(m, axis=0, keepdims=True)
    total = jnp.sum(tot[...].T * jnp.exp2(m - peak), axis=0, keepdims=True)
    out_ref[...] = jnp.broadcast_to(peak + jnp.log2(total), out_ref.shape)


def tree(op, xs):
    xs = list(xs)
    while len(xs) > 1:
        xs = [op(xs[i], xs[i + 1]) if i + 1 < len(xs) else xs[i] for i in range(0, len(xs), 2)]
    return xs[0]


def col_pass_kernel(log_b, part_ref, s_ref, out_ref, alpha_ref, wide):
    alpha = -combine(part_ref[...]) - log_b
    alpha_ref[...] = alpha
    wide[...] = jnp.broadcast_to(alpha, (LANES, alpha.shape[1])).T
    rows = s_ref.shape[0]
    piece = 256

    def group(c, carry):
        cols = pl.ds(pl.multiple_of(c * LANES, LANES), LANES)
        m = l = None
        for r in range(0, rows, piece):
            x = [s_ref[r + q:r + q + 8, cols] + wide[r + q:r + q + 8, :] for q in range(0, piece, 8)]
            top = tree(jnp.maximum, x)
            if m is None:
                m = top
                l = tree(jnp.add, [jnp.exp2(v - m) for v in x])
            else:
                new = jnp.maximum(m, top)
                l = l * jnp.exp2(m - new) + tree(jnp.add, [jnp.exp2(v - new) for v in x])
                m = new
        peak = jnp.max(m, axis=0, keepdims=True)
        total = jnp.sum(l * jnp.exp2(m - peak), axis=0, keepdims=True)
        out_ref[:, cols] = jnp.broadcast_to(peak + jnp.log2(total), (out_ref.shape[0], LANES))
        return carry

    lax.fori_loop(0, s_ref.shape[1] // LANES, group, 0)


def grad_kernel(log_a, log_b, part_ref, alpha_ref, a_ref, bhi_ref, blo_ref, s_ref, g_ref, beta_ref, awide, bwide, mass):
    beta = -combine(part_ref[...]) - log_a
    beta_ref[...] = beta
    bwide[...] = jnp.broadcast_to(beta + log_b, bwide.shape)
    awide[...] = jnp.broadcast_to(alpha_ref[...], (LANES, alpha_ref.shape[1])).T
    g_ref[...] = jnp.zeros_like(g_ref)
    mass[...] = jnp.zeros_like(mass)
    step, piece = 512, 256
    rows = s_ref.shape[0]

    def chunk(k, carry):
        at = pl.ds(pl.multiple_of(k * step, step), step)
        hi_b, lo_b = bhi_ref[at, :], blo_ref[at, :]
        right = jnp.concatenate([hi_b, lo_b, hi_b], axis=0)
        col = bwide[:, at][:1, :]
        for r in range(0, rows, piece):
            alpha = awide[r:r + piece, :]
            p = jnp.exp2(s_ref[r:r + piece, at] + jnp.concatenate([alpha] * (step // LANES), axis=1) + col)
            mass[r:r + piece, :] += tree(jnp.add, [p[:, q:q + LANES] for q in range(0, step, LANES)])
            hi, lo = split(p)
            left = jnp.concatenate([hi, hi, lo], axis=1)
            g_ref[r:r + piece, :] += jnp.dot(left, right, preferred_element_type=jnp.float32)
        return carry

    lax.fori_loop(0, s_ref.shape[1] // step, chunk, 0)
    total = jnp.sum(mass[...], axis=1, keepdims=True)
    g_ref[...] = 2.0 * (a_ref[...] * total - g_ref[...])


VM = pl.BlockSpec(memory_space=pltpu.VMEM)


def call(kernel, outs, scratch, *args, limit):
    return pl.pallas_call(
        kernel,
        out_shape=outs,
        in_specs=[VM] * len(args),
        out_specs=[VM] * len(outs),
        scratch_shapes=scratch,
        compiler_params=pltpu.CompilerParams(vmem_limit_bytes=limit),
    )(*args)


def f32(*shape):
    return jax.ShapeDtypeStruct(shape, jnp.float32)


def v16(*shape):
    return pltpu.VMEM(shape, jnp.bfloat16)


def v32(*shape):
    return pltpu.VMEM(shape, jnp.float32)


def spread(x, axis):
    return lax.all_to_all(x, axis, 0, 0, tiled=True)


def gather_a(points_a):
    size = lax.axis_size("ba")
    wide = jnp.broadcast_to(points_a[None], (size,) + points_a.shape)
    return lax.all_to_all(wide, "ba", 0, 0, tiled=True).reshape(size * points_a.shape[0], -1)


def gather_b(points_b):
    size = lax.axis_size("aa")
    rows = points_b.shape[0]
    half = rows // 2

    def move(x, by):
        return lax.ppermute(x, "aa", [(i, (i + 2 * by) % size) for i in range(size)])

    def swap(x):
        return lax.ppermute(x, "aa", [(i, i ^ 1) for i in range(size)])

    def place(by, flip, start):
        return lambda me: lax.rem(lax.bitwise_xor(me, flip) + 2 * by, size) * rows + start

    up, down = move(points_b, 1), move(points_b, -1)
    low, high = move(up[:half], 1), move(down[half:], -1)
    kept = [(points_b, 0, 0), (up, 3, 0), (down, 1, 0), (low, 2, 0), (high, 2, half)]
    pieces = [x for x, by, start in kept] + [swap(x) for x, by, start in kept]
    places = [place(by, flip, start) for flip in (0, 1) for x, by, start in kept]
    return pieces, places


def body(points_a, points_b):
    pieces, places = gather_b(points_b)
    return compute(gather_a(points_a), pieces, places, spread)


def compute(whole_a, pieces, places, spread):
    rows_a, width = whole_a.shape
    rows_b = sum(x.shape[0] for x in pieces)
    na, nb = lax.axis_size("aa"), lax.axis_size("ba")
    eps = width / 8.0
    log_a = -math.log2(rows_a * na)
    log_b = -math.log2(rows_b * nb)
    s, bhi, blo, a2, b2 = call(
        lambda *r: scores_kernel(eps, places, *r),
        [v32(rows_a, rows_b), v16(rows_b, width), v16(rows_b, width), f32(1, rows_a), f32(1, rows_b)],
        [v16(rows_a, 3 * width)],
        whole_a, *pieces, limit=16 * MIB)
    part = jnp.zeros((na, rows_b), jnp.float32)
    for turn in range(ITERS):
        rows, beta = call(
            lambda *r, first=turn == 0: row_pass_kernel(log_a, first, *r),
            [f32(nb, rows_a), f32(1, rows_b)],
            [v32(8, rows_b), v32(rows_a, LANES), v32(rows_a, LANES)],
            part, b2, s, limit=8 * MIB)
        cols, alpha = call(
            lambda *r: col_pass_kernel(log_b, *r),
            [f32(na, rows_b), f32(1, rows_a)],
            [v32(rows_a, LANES)],
            spread(rows, "ba"), s, limit=8 * MIB)
        part = spread(cols, "aa")
    g, beta = call(
        lambda *r: grad_kernel(log_a, log_b, *r),
        [f32(rows_a, width), f32(1, rows_b)],
        [v32(rows_a, LANES), v32(8, rows_b), v32(rows_a, LANES)],
        part, alpha, whole_a, bhi, blo, s, limit=12 * MIB)
    scale = eps / LOG2E
    pot_a = (scale * (alpha + a2)).reshape(rows_a)
    pot_b = (scale * (beta + b2)).reshape(rows_b)
    shares = lax.all_to_all(g.reshape(nb, rows_a // nb, width), "ba", 0, 0, tiled=True)
    return (pot_a, pot_b, jnp.sum(shares, axis=0))


def solution(mesh):
    placed = (P(("aa", "ba"), None), P(("ba", "aa"), None))
    return jax.shard_map(
        body,
        mesh=mesh,
        in_specs=placed,
        out_specs=(P("aa"), P("ba"), P(("aa", "ba"), None)),
        check_vma=False,
    )
```

```python
import math

import jax
import jax.numpy as jnp
from jax import lax
from jax.experimental import pallas as pl
from jax.experimental.pallas import tpu as pltpu
from jax.sharding import PartitionSpec as P

ITERS = 2
LOG2E = math.log2(math.e)
LANES = 128
MIB = 1024 * 1024


def split(x):
    hi = x.astype(jnp.bfloat16)
    return hi, (x - hi.astype(jnp.float32)).astype(jnp.bfloat16)


def row_norms(x):
    sq = x * x
    part = sq[:, :LANES]
    for k in range(LANES, sq.shape[1], LANES):
        part = part + sq[:, k:k + LANES]
    return jnp.sum(part.T, axis=0, keepdims=True)


def combine(parts):
    top = jnp.max(parts, axis=0, keepdims=True)
    return top + jnp.log2(jnp.sum(jnp.exp2(parts - top), axis=0, keepdims=True))


def prepare_kernel(eps, a_ref, left_ref, a2_ref):
    x = a_ref[...]
    a2_ref[...] = row_norms(x) * (LOG2E / eps)
    hi, lo = split(x * (2.0 * LOG2E / eps))
    left_ref[...] = jnp.concatenate([hi, hi, lo], axis=1)


def scores_kernel(eps, places, sizes, fresh, last, left, *refs):
    pieces, refs = refs[:sum(sizes)], refs[sum(sizes) + (0 if fresh else 6):]
    s_ref, bhi_ref, blo_ref, b2_ref, top_ref, tot_ref = refs[:6]
    me = lax.axis_index("aa")
    dims = (((1,), (1,)), ((), ()))
    for place, size in zip(places, sizes):
        y = jnp.concatenate([ref[...] for ref in pieces[:size]], axis=0)
        pieces = pieces[size:]
        at = pl.ds(pl.multiple_of(place(me), y.shape[0]), y.shape[0])
        norms = row_norms(y) * (LOG2E / eps)
        b2_ref[:, at] = norms
        hi, lo = split(y)
        bhi_ref[at, :] = hi
        blo_ref[at, :] = lo
        right = jnp.concatenate([hi, lo, hi], axis=1)
        x = lax.dot_general(left[...], right, dims, preferred_element_type=jnp.float32)
        s_ref[:, at] = x
        x = x - norms
        parts = [x[:, k:k + LANES] for k in range(0, y.shape[0], LANES)]
        top = tree(jnp.maximum, parts)
        if fresh:
            tot_ref[...] = tree(jnp.add, [jnp.exp2(v - top) for v in parts])
        else:
            old = top_ref[...]
            top = jnp.maximum(old, top)
            tot_ref[...] = tot_ref[...] * jnp.exp2(old - top) + tree(jnp.add, [jnp.exp2(v - top) for v in parts])
        top_ref[...] = top
        fresh = False
    if last:
        finish_rows(top_ref, tot_ref, refs[6])


def finish_rows(top_ref, tot_ref, out_ref):
    m = top_ref[...].T
    peak = jnp.max(m, axis=0, keepdims=True)
    total = jnp.sum(tot_ref[...].T * jnp.exp2(m - peak), axis=0, keepdims=True)
    out_ref[...] = jnp.broadcast_to(peak + jnp.log2(total), out_ref.shape)


def row_pass_kernel(log_a, part_ref, s_ref, out_ref, wide, top, tot):
    wide[...] = jnp.broadcast_to(-combine(part_ref[...]) - log_a, wide.shape)
    cols = s_ref.shape[1] // LANES

    def group(r, carry):
        rows = pl.ds(pl.multiple_of(r * 8, 8), 8)
        m, l = None, None
        for half in range(0, cols, 16):
            x = [s_ref[rows, k * LANES:(k + 1) * LANES] + wide[:, k * LANES:(k + 1) * LANES]
                 for k in range(half, min(cols, half + 16))]
            m, l = online(m, l, x)
        top[rows, :] = m
        tot[rows, :] = l
        return carry

    lax.fori_loop(0, s_ref.shape[0] // 8, group, 0, unroll=8)
    finish_rows(top, tot, out_ref)


def online(m, l, x):
    top = tree(jnp.maximum, x)
    if m is None:
        return top, tree(jnp.add, [jnp.exp2(v - top) for v in x])
    new = jnp.maximum(m, top)
    return new, l * jnp.exp2(m - new) + tree(jnp.add, [jnp.exp2(v - new) for v in x])


def tree(op, xs):
    xs = list(xs)
    while len(xs) > 1:
        xs = [op(xs[i], xs[i + 1]) if i + 1 < len(xs) else xs[i] for i in range(0, len(xs), 2)]
    return xs[0]


def col_pass_kernel(log_b, part_ref, s_ref, out_ref, alpha_ref, wide):
    alpha = -combine(part_ref[...]) - log_b
    alpha_ref[...] = alpha
    wide[...] = jnp.broadcast_to(alpha, (LANES, alpha.shape[1])).T
    rows = s_ref.shape[0]
    piece, across = 64, 8

    def group(c, carry):
        cols = [pl.ds(pl.multiple_of((c * across + k) * LANES, LANES), LANES) for k in range(across)]
        m, l = [None] * across, [None] * across
        for r in range(0, rows, piece):
            shift = [wide[r + q:r + q + 8, :] for q in range(0, piece, 8)]
            for k in range(across):
                x = [s_ref[r + q:r + q + 8, cols[k]] + shift[q // 8] for q in range(0, piece, 8)]
                m[k], l[k] = online(m[k], l[k], x)
        for k in range(across):
            peak = jnp.max(m[k], axis=0, keepdims=True)
            total = jnp.sum(l[k] * jnp.exp2(m[k] - peak), axis=0, keepdims=True)
            out_ref[:, cols[k]] = jnp.broadcast_to(peak + jnp.log2(total), (out_ref.shape[0], LANES))
        return carry

    lax.fori_loop(0, s_ref.shape[1] // (LANES * across), group, 0)


def grad_kernel(log_a, log_b, start, part_ref, alpha_ref, a_ref, bhi_ref, blo_ref, s_ref, g_ref, beta_ref, awide, bwide, mass, acc):
    beta = -combine(part_ref[...]) - log_a
    beta_ref[...] = beta
    bwide[...] = jnp.broadcast_to(beta + log_b, bwide.shape)
    awide[...] = jnp.broadcast_to(alpha_ref[...], (LANES, alpha_ref.shape[1])).T
    shares, n = g_ref.shape[:2]
    share = s_ref.shape[0] // shares
    step, group = 1024, 256 // n

    def take(ref, first, cols):
        return jnp.concatenate([ref[pl.ds(d * share + start, n), cols] for d in range(first, first + group)], axis=0)

    def chunk(k, begin):
        at = pl.ds(pl.multiple_of(k * step, step), step)
        hi_b, lo_b = bhi_ref[at, :], blo_ref[at, :]
        right = jnp.concatenate([hi_b, lo_b, hi_b], axis=0)
        col = bwide[:, at][:1, :]
        for first in range(0, shares, group):
            rows = slice(first * n, (first + group) * n)
            alpha = take(awide, first, slice(None))
            p = jnp.exp2(take(s_ref, first, at) + jnp.concatenate([alpha] * (step // LANES), axis=1) + col)
            part = tree(jnp.add, [p[:, q:q + LANES] for q in range(0, step, LANES)])
            hi, lo = split(p)
            left = jnp.concatenate([hi, hi, lo], axis=1)
            pulled = jnp.dot(left, right, preferred_element_type=jnp.float32)
            mass[rows, :] = part if begin else mass[rows, :] + part
            acc[rows, :] = pulled if begin else acc[rows, :] + pulled

    chunk(0, True)
    lax.fori_loop(1, s_ref.shape[1] // step, lambda k, carry: chunk(k, False), None)
    total = jnp.sum(mass[...], axis=1, keepdims=True)
    for d in range(shares):
        rows = slice(d * n, (d + 1) * n)
        g_ref[d] = 2.0 * (a_ref[pl.ds(d * share + start, n), :] * total[rows] - acc[rows, :])


VM = pl.BlockSpec(memory_space=pltpu.VMEM)


def call(kernel, outs, scratch, *args, limit=12 * MIB, aliases={}, cost=None):
    return pl.pallas_call(
        kernel,
        out_shape=outs,
        in_specs=[VM] * len(args),
        out_specs=[VM] * len(outs),
        scratch_shapes=scratch,
        input_output_aliases=aliases,
        cost_estimate=cost,
        compiler_params=pltpu.CompilerParams(vmem_limit_bytes=limit),
    )(*args)


def f32(*shape):
    return jax.ShapeDtypeStruct(shape, jnp.float32)


def v16(*shape):
    return pltpu.VMEM(shape, jnp.bfloat16)


def v32(*shape):
    return pltpu.VMEM(shape, jnp.float32)


def spread(x, axis):
    return lax.all_to_all(x, axis, 0, 0, tiled=True)


def gather_a(points_a):
    size = lax.axis_size("ba")
    wide = jnp.broadcast_to(points_a[None], (size,) + points_a.shape)
    return lax.all_to_all(wide, "ba", 0, 0, tiled=True).reshape(size * points_a.shape[0], -1)


def gather_b(points_b):
    size = lax.axis_size("aa")
    rows = points_b.shape[0]
    half = rows // 2

    def move(x, by):
        return lax.ppermute(x, "aa", [(i, (i + 2 * by) % size) for i in range(size)])

    def swap(x):
        return lax.ppermute(x, "aa", [(i, i ^ 1) for i in range(size)])

    def place(by, flip):
        return lambda me: lax.rem(lax.bitwise_xor(me, flip) + 2 * by, size) * rows

    up, down = move(points_b, 1), move(points_b, -1)
    low, high = move(up[:half], 1), move(down[half:], -1)
    def stage(*items):
        return [(pieces, place(by, flip)) for pieces, by, flip in items]

    up, down = move(points_b, 1), move(points_b, -1)
    low, high = move(up[:half], 1), move(down[half:], -1)
    return [
        stage(([points_b], 0, 0), ([swap(points_b)], 0, 1)),
        stage(([up], 3, 0), ([down], 1, 0)),
        stage(([swap(up)], 3, 1), ([swap(down)], 1, 1)),
        stage(([low, high], 2, 0), ([swap(low), swap(high)], 2, 1)),
    ]


def body(points_a, points_b):
    stages = gather_b(points_b)
    whole_a = gather_a(points_a)
    rows_a, width = whole_a.shape
    na, nb = lax.axis_size("aa"), lax.axis_size("ba")
    rows_b = points_b.shape[0] * na
    eps = width / 8.0
    log_a = -math.log2(rows_a * na)
    log_b = -math.log2(rows_b * nb)
    left, a2 = call(lambda *r: prepare_kernel(eps, *r), [v16(rows_a, 3 * width), f32(1, rows_a)], [], whole_a)
    held = []
    for k, stage in enumerate(stages):
        places = [place for pieces, place in stage]
        sizes = [len(pieces) for pieces, place in stage]
        flat = [x for pieces, place in stage for x in pieces]
        last = k == len(stages) - 1
        outs = [v32(rows_a, rows_b), v16(rows_b, width), v16(rows_b, width), v32(1, rows_b), v32(rows_a, LANES), v32(rows_a, LANES)]
        held = call(
            lambda *r: scores_kernel(eps, places, sizes, k == 0, last, *r),
            outs + ([f32(nb, rows_a)] if last else []),
            [], left, *flat, *held,
            aliases={1 + len(flat) + i: i for i in range(len(held))},
            cost=pl.CostEstimate(flops=6 * rows_a * width * sum(x.shape[0] for x in flat), bytes_accessed=4 * MIB, transcendentals=0))
    s, bhi, blo, b2, _, _, rows = held
    for turn in range(ITERS):
        if turn > 0:
            rows, = call(
                lambda *r: row_pass_kernel(log_a, *r),
                [f32(nb, rows_a)],
                [v32(8, rows_b), v32(rows_a, LANES), v32(rows_a, LANES)],
                part, s)
        cols, alpha = call(
            lambda *r: col_pass_kernel(log_b, *r),
            [f32(na, rows_b), f32(1, rows_a)],
            [v32(rows_a, LANES)],
            spread(rows, "ba"), s)
        part = spread(cols, "aa")
    share = rows_a // nb
    cut = share // 2
    sums = []
    for start in range(0, share, cut):
        g, beta = call(
            lambda *r: grad_kernel(log_a, log_b, start, *r),
            [f32(nb, cut, width), f32(1, rows_b)],
            [v32(rows_a, LANES), v32(8, rows_b), v32(nb * cut, LANES), v32(nb * cut, width)],
            part, alpha, whole_a, bhi, blo, s,
            cost=pl.CostEstimate(flops=6 * nb * cut * width * rows_b, bytes_accessed=4 * MIB, transcendentals=0))
        sums.append(jnp.sum(spread(g, "ba"), axis=0))
    scale = eps / LOG2E
    pot_a = (scale * (alpha + a2)).reshape(rows_a)
    pot_b = (scale * (beta + b2)).reshape(rows_b)
    return (pot_a, pot_b, jnp.concatenate(sums, axis=0))


def solution(mesh):
    placed = (P(("aa", "ba"), None), P(("ba", "aa"), None))
    return jax.shard_map(
        body,
        mesh=mesh,
        in_specs=placed,
        out_specs=(P("aa"), P("ba"), P(("aa", "ba"), None)),
        check_vma=False,
    )
```

```python
import math

import jax
import jax.numpy as jnp
from jax import lax
from jax.experimental import pallas as pl
from jax.experimental.pallas import tpu as pltpu
from jax.sharding import PartitionSpec as P

ITERS = 2
LOG2E = math.log2(math.e)
LANES = 128
MIB = 1024 * 1024


def split(x):
    hi = x.astype(jnp.bfloat16)
    return hi, (x - hi.astype(jnp.float32)).astype(jnp.bfloat16)


def row_norms(x):
    sq = x * x
    part = sq[:, :LANES]
    for k in range(LANES, sq.shape[1], LANES):
        part = part + sq[:, k:k + LANES]
    return jnp.sum(part.T, axis=0, keepdims=True)


def combine(parts):
    top = jnp.max(parts, axis=0, keepdims=True)
    return top + jnp.log2(jnp.sum(jnp.exp2(parts - top), axis=0, keepdims=True))


def prepare_kernel(eps, a_ref, left_ref, a2_ref):
    x = a_ref[...]
    a2_ref[...] = row_norms(x) * (LOG2E / eps)
    hi, lo = split(x * (2.0 * LOG2E / eps))
    left_ref[...] = jnp.concatenate([hi, hi, lo], axis=1)


def scores_kernel(eps, places, sizes, fresh, last, left, *refs):
    pieces, refs = refs[:sum(sizes)], refs[sum(sizes) + (0 if fresh else 6):]
    s_ref, bhi_ref, blo_ref, b2_ref, top_ref, tot_ref = refs[:6]
    me = lax.axis_index("aa")
    dims = (((1,), (1,)), ((), ()))
    for place, size in zip(places, sizes):
        y = jnp.concatenate([ref[...] for ref in pieces[:size]], axis=0)
        pieces = pieces[size:]
        at = pl.ds(pl.multiple_of(place(me), y.shape[0]), y.shape[0])
        norms = row_norms(y) * (LOG2E / eps)
        b2_ref[:, at] = norms
        hi, lo = split(y)
        bhi_ref[at, :] = hi
        blo_ref[at, :] = lo
        right = jnp.concatenate([hi, lo, hi], axis=1)
        x = lax.dot_general(left[...], right, dims, preferred_element_type=jnp.float32)
        s_ref[:, at] = x
        x = x - norms
        parts = [x[:, k:k + LANES] for k in range(0, y.shape[0], LANES)]
        top = tree(jnp.maximum, parts)
        if fresh:
            tot_ref[...] = tree(jnp.add, [jnp.exp2(v - top) for v in parts])
        else:
            old = top_ref[...]
            top = jnp.maximum(old, top)
            tot_ref[...] = tot_ref[...] * jnp.exp2(old - top) + tree(jnp.add, [jnp.exp2(v - top) for v in parts])
        top_ref[...] = top
        fresh = False
    if last:
        finish_rows(top_ref, tot_ref, refs[6])


def finish_rows(top_ref, tot_ref, out_ref):
    m = top_ref[...].T
    peak = jnp.max(m, axis=0, keepdims=True)
    total = jnp.sum(tot_ref[...].T * jnp.exp2(m - peak), axis=0, keepdims=True)
    out_ref[...] = jnp.broadcast_to(peak + jnp.log2(total), out_ref.shape)


def row_pass_kernel(log_a, part_ref, s_ref, out_ref, wide, top, tot):
    wide[...] = jnp.broadcast_to(-combine(part_ref[...]) - log_a, wide.shape)
    cols = s_ref.shape[1] // LANES

    def group(r, carry):
        rows = pl.ds(pl.multiple_of(r * 8, 8), 8)
        m, l = None, None
        for half in range(0, cols, 16):
            x = [s_ref[rows, k * LANES:(k + 1) * LANES] + wide[:, k * LANES:(k + 1) * LANES]
                 for k in range(half, min(cols, half + 16))]
            m, l = online(m, l, x)
        top[rows, :] = m
        tot[rows, :] = l
        return carry

    lax.fori_loop(0, s_ref.shape[0] // 8, group, 0, unroll=8)
    finish_rows(top, tot, out_ref)


def online(m, l, x):
    top = tree(jnp.maximum, x)
    if m is None:
        return top, tree(jnp.add, [jnp.exp2(v - top) for v in x])
    new = jnp.maximum(m, top)
    return new, l * jnp.exp2(m - new) + tree(jnp.add, [jnp.exp2(v - new) for v in x])


def tree(op, xs):
    xs = list(xs)
    while len(xs) > 1:
        xs = [op(xs[i], xs[i + 1]) if i + 1 < len(xs) else xs[i] for i in range(0, len(xs), 2)]
    return xs[0]


def col_pass_kernel(log_b, eps, part_ref, a2_ref, s_ref, out_ref, alpha_ref, pot_ref, wide):
    alpha = -combine(part_ref[...]) - log_b
    alpha_ref[...] = alpha
    pot_ref[...] = (alpha + a2_ref[...]) * (eps / LOG2E)
    wide[...] = jnp.broadcast_to(alpha, (LANES, alpha.shape[1])).T
    rows = s_ref.shape[0]
    piece, across = 64, 8

    def group(c, carry):
        cols = [pl.ds(pl.multiple_of((c * across + k) * LANES, LANES), LANES) for k in range(across)]
        m, l = [None] * across, [None] * across
        for r in range(0, rows, piece):
            shift = [wide[r + q:r + q + 8, :] for q in range(0, piece, 8)]
            for k in range(across):
                x = [s_ref[r + q:r + q + 8, cols[k]] + shift[q // 8] for q in range(0, piece, 8)]
                m[k], l[k] = online(m[k], l[k], x)
        for k in range(across):
            peak = jnp.max(m[k], axis=0, keepdims=True)
            total = jnp.sum(l[k] * jnp.exp2(m[k] - peak), axis=0, keepdims=True)
            out_ref[:, cols[k]] = jnp.broadcast_to(peak + jnp.log2(total), (out_ref.shape[0], LANES))
        return carry

    lax.fori_loop(0, s_ref.shape[1] // (LANES * across), group, 0)


def weights_kernel(log_a, log_b, eps, part_ref, alpha_ref, b2_ref, awide_ref, bwide_ref, pot_ref):
    beta = -combine(part_ref[...]) - log_a
    pot_ref[...] = (beta + b2_ref[...]) * (eps / LOG2E)
    bwide_ref[...] = jnp.broadcast_to(beta + log_b, bwide_ref.shape)
    awide_ref[...] = jnp.broadcast_to(alpha_ref[...], (LANES, alpha_ref.shape[1])).T


def grad_kernel(first, awide_ref, bwide_ref, a_ref, bhi_ref, blo_ref, s_ref, g_ref, mass):
    n = g_ref.shape[0]
    rows = pl.ds(pl.multiple_of(first(), n), n)
    step = 1024

    def chunk(k, begin):
        at = pl.ds(pl.multiple_of(k * step, step), step)
        hi_b, lo_b = bhi_ref[at, :], blo_ref[at, :]
        right = jnp.concatenate([hi_b, lo_b, hi_b], axis=0)
        alpha = awide_ref[rows, :]
        p = jnp.exp2(s_ref[rows, at] + jnp.concatenate([alpha] * (step // LANES), axis=1) + bwide_ref[:, at][:1, :])
        part = tree(jnp.add, [p[:, q:q + LANES] for q in range(0, step, LANES)])
        hi, lo = split(p)
        left = jnp.concatenate([hi, hi, lo], axis=1)
        pulled = jnp.dot(left, right, preferred_element_type=jnp.float32)
        mass[...] = part if begin else mass[...] + part
        g_ref[...] = pulled if begin else g_ref[...] + pulled

    chunk(0, True)
    lax.fori_loop(1, s_ref.shape[1] // step, lambda k, carry: chunk(k, False), None)
    g_ref[...] = 2.0 * (a_ref[rows, :] * jnp.sum(mass[...], axis=1, keepdims=True) - g_ref[...])


def turn_sum_kernel(order, *refs):
    parts, outs = refs[:2], refs[2:]
    n = outs[0].shape[0]
    for out_ref, first in zip(outs, order()):
        rows = pl.ds(pl.multiple_of(first * n, n), n)
        out_ref[...] = tree(jnp.add, [part[rows, :] for part in parts])


def sum_kernel(*refs):
    refs[-1][...] = tree(jnp.add, [part[...] for part in refs[:-1]])


VM = pl.BlockSpec(memory_space=pltpu.VMEM)


def call(kernel, outs, scratch, *args, limit=6 * MIB, aliases={}, cost=None):
    return pl.pallas_call(
        kernel,
        out_shape=outs,
        in_specs=[VM] * len(args),
        out_specs=[VM] * len(outs),
        scratch_shapes=scratch,
        input_output_aliases=aliases,
        cost_estimate=cost,
        compiler_params=pltpu.CompilerParams(vmem_limit_bytes=limit),
    )(*args)


def f32(*shape):
    return jax.ShapeDtypeStruct(shape, jnp.float32)


def v16(*shape):
    return pltpu.VMEM(shape, jnp.bfloat16)


def v32(*shape):
    return pltpu.VMEM(shape, jnp.float32)


def spread(x, axis):
    return lax.all_to_all(x, axis, 0, 0, tiled=True)


def body(points_a, points_b):
    na, nb = lax.axis_size("aa"), lax.axis_size("ba")
    share, width = points_a.shape
    piece = points_b.shape[0]
    rows_a, rows_b = share * nb, piece * na
    eps = width / 8.0
    log_a = -math.log2(rows_a * na)
    log_b = -math.log2(rows_b * nb)

    def move(x, by):
        return lax.ppermute(x, "aa", [(i, (i + 2 * by) % na) for i in range(na)])

    def swap(x):
        return lax.ppermute(x, "aa", [(i, i ^ 1) for i in range(na)])

    def place(by, flip):
        return lambda me: lax.rem(lax.bitwise_xor(me, flip) + 2 * by, na) * piece

    half = piece // 2
    up, down = move(points_b, 1), move(points_b, -1)
    low, high = move(up[:half], 1), move(down[half:], -1)
    wide = jnp.broadcast_to(points_a[None], (nb, share, width))
    whole_a = spread(wide, "ba").reshape(rows_a, width)
    stages = [
        [([points_b], place(0, 0)), ([swap(points_b)], place(0, 1)),
         ([up], place(3, 0)), ([down], place(1, 0)), ([swap(up)], place(3, 1)), ([swap(down)], place(1, 1)),
         ([low, high], place(2, 0)), ([swap(low), swap(high)], place(2, 1))],
    ]
    left, a2 = call(lambda *r: prepare_kernel(eps, *r), [v16(rows_a, 3 * width), v32(1, rows_a)], [], whole_a)
    held = []
    for k, stage in enumerate(stages):
        places = [place for pieces, place in stage]
        sizes = [len(pieces) for pieces, place in stage]
        flat = [x for pieces, place in stage for x in pieces]
        last = k == len(stages) - 1
        outs = [v32(rows_a, rows_b), v16(rows_b, width), v16(rows_b, width), v32(1, rows_b), v32(rows_a, LANES), v32(rows_a, LANES)]
        held = call(
            lambda *r: scores_kernel(eps, places, sizes, k == 0, last, *r),
            outs + ([v32(nb, rows_a)] if last else []),
            [], left, *flat, *held, limit=12 * MIB,
            aliases={1 + len(flat) + i: i for i in range(len(held))},
            cost=pl.CostEstimate(flops=6 * rows_a * width * sum(x.shape[0] for x in flat), bytes_accessed=4 * MIB, transcendentals=0))
    s, bhi, blo, b2, _, _, rows = held
    for turn in range(ITERS):
        if turn > 0:
            rows, = call(
                lambda *r: row_pass_kernel(log_a, *r),
                [f32(nb, rows_a)],
                [v32(8, rows_b), v32(rows_a, LANES), v32(rows_a, LANES)],
                part, s)
        cols, alpha, pot_a = call(
            lambda *r: col_pass_kernel(log_b, eps, *r),
            [f32(na, rows_b), v32(1, rows_a), f32(1, rows_a)],
            [v32(rows_a, LANES)],
            spread(rows, "ba"), a2, s)
        part = spread(cols, "aa")
    awide, bwide, pot_b = call(
        lambda *r: weights_kernel(log_a, log_b, eps, *r),
        [v32(rows_a, LANES), v32(8, rows_b), f32(1, rows_b)], [], part, alpha, b2)

    def along_x(v, by):
        return lax.ppermute(v, "ba", [(i, (i + side * by) % nb) for i in range(nb)])

    def along_y(v, by):
        return lax.ppermute(v, "ba", [(i, i // side * side + (i + by) % side) for i in range(nb)])

    side = math.isqrt(nb)
    step = pl.CostEstimate(flops=6 * rows_a // side * width * rows_b, bytes_accessed=4 * MIB, transcendentals=0)
    held = []
    for by in [*range(1, side), 0]:
        g, = call(
            lambda *r: grad_kernel(lambda: lax.rem(lax.axis_index("ba") // side + by, side) * (rows_a // side), *r),
            [v32(rows_a // side, width)], [v32(rows_a // side, LANES)],
            awide, bwide, whole_a, bhi, blo, s,
            cost=step)
        held.append(along_x(g, by) if by else g)
    *arrived, total = held
    for g in arrived[:-1]:
        total, = call(sum_kernel, [v32(rows_a // side, width)], [], total, g, cost=step)
    cuts = call(
        lambda *r: turn_sum_kernel(lambda: [lax.rem(lax.rem(lax.axis_index("ba"), side) + by, side) for by in range(side)], *r),
        [v32(share, width)] * side, [], total, arrived[-1])
    grad, = call(sum_kernel, [f32(share, width)], [], cuts[0], *[along_y(cuts[by], by) for by in range(1, side)])
    return (pot_a.reshape(rows_a), pot_b.reshape(rows_b), grad)


def solution(mesh):
    placed = (P(("aa", "ba"), None), P(("ba", "aa"), None))
    return jax.shard_map(
        body,
        mesh=mesh,
        in_specs=placed,
        out_specs=(P("aa"), P("ba"), P(("aa", "ba"), None)),
        check_vma=False,
    )
```

```python
import math

import jax
import jax.numpy as jnp
from jax import lax
from jax.experimental import pallas as pl
from jax.experimental.pallas import tpu as pltpu
from jax.sharding import PartitionSpec as P

ITERS = 2
LOG2E = math.log2(math.e)
LANES = 128
MIB = 1024 * 1024


def split(x):
    hi = x.astype(jnp.bfloat16)
    return hi, (x - hi.astype(jnp.float32)).astype(jnp.bfloat16)


def row_norms(x):
    sq = x * x
    part = sq[:, :LANES]
    for k in range(LANES, sq.shape[1], LANES):
        part = part + sq[:, k:k + LANES]
    return jnp.sum(part.T, axis=0, keepdims=True)


def combine(parts):
    top = jnp.max(parts, axis=0, keepdims=True)
    return top + jnp.log2(jnp.sum(jnp.exp2(parts - top), axis=0, keepdims=True))


def repeat_kernel(a_ref, out_ref):
    for d in range(out_ref.shape[0]):
        out_ref[d] = a_ref[...]


def prepare_kernel(eps, a_ref, left_ref, a2_ref):
    x = a_ref[...]
    a2_ref[...] = row_norms(x) * (LOG2E / eps)
    hi, lo = split(x * (2.0 * LOG2E / eps))
    left_ref[...] = jnp.concatenate([hi, hi, lo], axis=1)


def pieces_kernel(eps, places, *refs):
    pieces, (bhi_ref, blo_ref, b2_ref) = refs[:len(places)], refs[-3:]
    me = lax.axis_index("aa")
    for ref, place in zip(pieces, places):
        y = ref[...]
        at = pl.ds(pl.multiple_of(place(me), y.shape[0]), y.shape[0])
        b2_ref[:, at] = row_norms(y) * (LOG2E / eps)
        bhi_ref[at, :], blo_ref[at, :] = split(y)


def scores_kernel(n, left, bhi_ref, blo_ref, b2_ref, s_ref, out_ref, top_ref, tot_ref):
    for start in range(0, s_ref.shape[1], n):
        at = pl.ds(start, n)
        hi, lo = bhi_ref[at, :], blo_ref[at, :]
        right = jnp.concatenate([hi, lo, hi], axis=1)
        x = lax.dot_general(left[...], right, (((1,), (1,)), ((), ())), preferred_element_type=jnp.float32)
        s_ref[:, at] = x
        x = x - b2_ref[:, at]
        parts = [x[:, k:k + LANES] for k in range(0, n, LANES)]
        top = tree(jnp.maximum, parts)
        if start == 0:
            tot_ref[...] = tree(jnp.add, [jnp.exp2(v - top) for v in parts])
        else:
            old = top_ref[...]
            top = jnp.maximum(old, top)
            tot_ref[...] = tot_ref[...] * jnp.exp2(old - top) + tree(jnp.add, [jnp.exp2(v - top) for v in parts])
        top_ref[...] = top
    finish_rows(top_ref, tot_ref, out_ref)


def finish_rows(top_ref, tot_ref, out_ref):
    m = top_ref[...].T
    peak = jnp.max(m, axis=0, keepdims=True)
    total = jnp.sum(tot_ref[...].T * jnp.exp2(m - peak), axis=0, keepdims=True)
    out_ref[...] = jnp.broadcast_to(peak + jnp.log2(total), out_ref.shape)


def row_pass_kernel(log_a, part_ref, s_ref, out_ref, wide, top, tot):
    wide[...] = jnp.broadcast_to(-combine(part_ref[...]) - log_a, wide.shape)
    cols = s_ref.shape[1] // LANES

    def group(r, carry):
        rows = pl.ds(pl.multiple_of(r * 8, 8), 8)
        m, l = None, None
        for half in range(0, cols, 16):
            x = [s_ref[rows, k * LANES:(k + 1) * LANES] + wide[:, k * LANES:(k + 1) * LANES]
                 for k in range(half, min(cols, half + 16))]
            m, l = online(m, l, x)
        top[rows, :] = m
        tot[rows, :] = l
        return carry

    lax.fori_loop(0, s_ref.shape[0] // 8, group, 0, unroll=8)
    finish_rows(top, tot, out_ref)


def online(m, l, x):
    top = tree(jnp.maximum, x)
    if m is None:
        return top, tree(jnp.add, [jnp.exp2(v - top) for v in x])
    new = jnp.maximum(m, top)
    return new, l * jnp.exp2(m - new) + tree(jnp.add, [jnp.exp2(v - new) for v in x])


def tree(op, xs):
    xs = list(xs)
    while len(xs) > 1:
        xs = [op(xs[i], xs[i + 1]) if i + 1 < len(xs) else xs[i] for i in range(0, len(xs), 2)]
    return xs[0]


def col_pass_kernel(log_b, eps, part_ref, a2_ref, s_ref, out_ref, alpha_ref, pot_ref, wide):
    alpha = -combine(part_ref[...]) - log_b
    alpha_ref[...] = alpha
    pot_ref[...] = (alpha + a2_ref[...]) * (eps / LOG2E)
    wide[...] = jnp.broadcast_to(alpha, (LANES, alpha.shape[1])).T
    rows = s_ref.shape[0]
    piece, across = 64, 8

    def group(c, carry):
        cols = [pl.ds(pl.multiple_of((c * across + k) * LANES, LANES), LANES) for k in range(across)]
        m, l = [None] * across, [None] * across
        for r in range(0, rows, piece):
            shift = [wide[r + q:r + q + 8, :] for q in range(0, piece, 8)]
            for k in range(across):
                x = [s_ref[r + q:r + q + 8, cols[k]] + shift[q // 8] for q in range(0, piece, 8)]
                m[k], l[k] = online(m[k], l[k], x)
        for k in range(across):
            peak = jnp.max(m[k], axis=0, keepdims=True)
            total = jnp.sum(l[k] * jnp.exp2(m[k] - peak), axis=0, keepdims=True)
            out_ref[:, cols[k]] = jnp.broadcast_to(peak + jnp.log2(total), (out_ref.shape[0], LANES))
        return carry

    lax.fori_loop(0, s_ref.shape[1] // (LANES * across), group, 0)


def weights_kernel(log_a, log_b, eps, part_ref, alpha_ref, b2_ref, awide_ref, bwide_ref, pot_ref):
    beta = -combine(part_ref[...]) - log_a
    pot_ref[...] = (beta + b2_ref[...]) * (eps / LOG2E)
    bwide_ref[...] = jnp.broadcast_to(beta + log_b, bwide_ref.shape)
    awide_ref[...] = jnp.broadcast_to(alpha_ref[...], (LANES, alpha_ref.shape[1])).T


def grad_kernel(first, awide_ref, bwide_ref, a_ref, bhi_ref, blo_ref, s_ref, g_ref, mass):
    n = g_ref.shape[0]
    rows = pl.ds(pl.multiple_of(first(), n), n)
    step = 1024

    for start in range(0, s_ref.shape[1], step):
        at = pl.ds(start, step)
        hi_b, lo_b = bhi_ref[at, :], blo_ref[at, :]
        right = jnp.concatenate([hi_b, lo_b, hi_b], axis=0)
        alpha = awide_ref[rows, :]
        p = jnp.exp2(s_ref[rows, at] + jnp.concatenate([alpha] * (step // LANES), axis=1) + bwide_ref[:, at][:1, :])
        part = tree(jnp.add, [p[:, q:q + LANES] for q in range(0, step, LANES)])
        hi, lo = split(p)
        left = jnp.concatenate([hi, hi, lo], axis=1)
        pulled = jnp.dot(left, right, preferred_element_type=jnp.float32)
        mass[...] = part if start == 0 else mass[...] + part
        g_ref[...] = pulled if start == 0 else g_ref[...] + pulled
    g_ref[...] = 2.0 * (a_ref[rows, :] * jnp.sum(mass[...], axis=1, keepdims=True) - g_ref[...])


def turn_sum_kernel(order, *refs):
    parts, outs = refs[:2], refs[2:]
    n = outs[0].shape[0]
    for out_ref, first in zip(outs, order()):
        rows = pl.ds(pl.multiple_of(first * n, n), n)
        out_ref[...] = tree(jnp.add, [part[rows, :] for part in parts])


def sum_kernel(*refs):
    refs[-1][...] = tree(jnp.add, [part[...] for part in refs[:-1]])


VM = pl.BlockSpec(memory_space=pltpu.VMEM)


def call(kernel, outs, scratch, *args, limit=6 * MIB, aliases={}, cost=None):
    return pl.pallas_call(
        kernel,
        out_shape=outs,
        in_specs=[VM] * len(args),
        out_specs=[VM] * len(outs),
        scratch_shapes=scratch,
        input_output_aliases=aliases,
        cost_estimate=cost,
        compiler_params=pltpu.CompilerParams(vmem_limit_bytes=limit),
    )(*args)


def f32(*shape):
    return jax.ShapeDtypeStruct(shape, jnp.float32)


def v16(*shape):
    return pltpu.VMEM(shape, jnp.bfloat16)


def v32(*shape):
    return pltpu.VMEM(shape, jnp.float32)


def spread(x, axis):
    return lax.all_to_all(x, axis, 0, 0, tiled=True)


def body(points_a, points_b):
    na, nb = lax.axis_size("aa"), lax.axis_size("ba")
    share, width = points_a.shape
    piece = points_b.shape[0]
    rows_a, rows_b = share * nb, piece * na
    eps = width / 8.0
    log_a = -math.log2(rows_a * na)
    log_b = -math.log2(rows_b * nb)

    def move(x, by):
        return lax.ppermute(x, "aa", [(i, (i + 2 * by) % na) for i in range(na)])

    def swap(x):
        return lax.ppermute(x, "aa", [(i, i ^ 1) for i in range(na)])

    def place(by, flip, start=0):
        return lambda me: lax.rem(lax.bitwise_xor(me, flip) + 2 * by, na) * piece + start

    half = piece // 2
    up, down = move(points_b, 1), move(points_b, -1)
    low, high = move(up[:half], 1), move(down[half:], -1)
    wide, = call(repeat_kernel, [f32(nb, share, width)], [], points_a)
    whole_a = spread(wide, "ba").reshape(rows_a, width)
    pieces = [
        (points_b, place(0, 0)), (up, place(3, 0)), (down, place(1, 0)), (low, place(2, 0)), (high, place(2, 0, half)),
        (swap(points_b), place(0, 1)), (swap(up), place(3, 1)), (swap(down), place(1, 1)),
        (swap(low), place(2, 1)), (swap(high), place(2, 1, half))]
    bhi, blo, b2 = call(
        lambda *r: pieces_kernel(eps, [p for x, p in pieces], *r),
        [v16(rows_b, width), v16(rows_b, width), v32(1, rows_b)], [], *[x for x, p in pieces],
        cost=pl.CostEstimate(flops=0, bytes_accessed=64 * MIB, transcendentals=0))
    left, a2 = call(lambda *r: prepare_kernel(eps, *r), [v16(rows_a, 3 * width), v32(1, rows_a)], [], whole_a)
    s, rows = call(
        lambda *r: scores_kernel(piece, *r),
        [v32(rows_a, rows_b), v32(nb, rows_a)], [v32(rows_a, LANES), v32(rows_a, LANES)],
        left, bhi, blo, b2, limit=8 * MIB)
    for turn in range(ITERS):
        if turn > 0:
            rows, = call(
                lambda *r: row_pass_kernel(log_a, *r),
                [f32(nb, rows_a)],
                [v32(8, rows_b), v32(rows_a, LANES), v32(rows_a, LANES)],
                part, s)
        cols, alpha, pot_a = call(
            lambda *r: col_pass_kernel(log_b, eps, *r),
            [f32(na, rows_b), v32(1, rows_a), f32(1, rows_a)],
            [v32(rows_a, LANES)],
            spread(rows, "ba"), a2, s)
        part = spread(cols, "aa")
    awide, bwide, pot_b = call(
        lambda *r: weights_kernel(log_a, log_b, eps, *r),
        [v32(rows_a, LANES), v32(8, rows_b), f32(1, rows_b)], [], part, alpha, b2)

    def along_x(v, by):
        return lax.ppermute(v, "ba", [(i, (i + side * by) % nb) for i in range(nb)])

    def along_y(v, by):
        return lax.ppermute(v, "ba", [(i, i // side * side + (i + by) % side) for i in range(nb)])

    side = math.isqrt(nb)
    step = pl.CostEstimate(flops=2 * rows_a // side * width * rows_b, bytes_accessed=MIB, transcendentals=0)
    held = []
    for by in [*range(1, side), 0]:
        g, = call(
            lambda *r: grad_kernel(lambda: lax.rem(lax.axis_index("ba") // side + by, side) * (rows_a // side), *r),
            [v32(rows_a // side, width)], [v32(rows_a // side, LANES)],
            awide, bwide, whole_a, bhi, blo, s, limit=12 * MIB, cost=step)
        held.append(along_x(g, by) if by else g)
    *arrived, total = held
    long = pl.CostEstimate(flops=9 * step.flops, bytes_accessed=4 * MIB, transcendentals=0)
    for g in arrived[:-1]:
        total, = call(sum_kernel, [v32(rows_a // side, width)], [], total, g, cost=long)
    cuts = call(
        lambda *r: turn_sum_kernel(lambda: [lax.rem(lax.rem(lax.axis_index("ba"), side) + by, side) for by in range(side)], *r),
        [v32(share, width)] * side, [], total, arrived[-1])
    grad, = call(sum_kernel, [f32(share, width)], [], cuts[0], *[along_y(cuts[by], by) for by in range(1, side)])
    return (pot_a.reshape(rows_a), pot_b.reshape(rows_b), grad)


def solution(mesh):
    placed = (P(("aa", "ba"), None), P(("ba", "aa"), None))
    return jax.shard_map(
        body,
        mesh=mesh,
        in_specs=placed,
        out_specs=(P("aa"), P("ba"), P(("aa", "ba"), None)),
        check_vma=False,
    )
```

```python
import math

import jax
import jax.numpy as jnp
from jax import lax
from jax.experimental import pallas as pl
from jax.experimental.pallas import tpu as pltpu
from jax.sharding import PartitionSpec as P

ITERS = 2
LOG2E = math.log2(math.e)
LANES = 128
MIB = 1024 * 1024


def split(x):
    hi = x.astype(jnp.bfloat16)
    return hi, (x - hi.astype(jnp.float32)).astype(jnp.bfloat16)


def row_norms(x):
    sq = x * x
    part = sq[:, :LANES]
    for k in range(LANES, sq.shape[1], LANES):
        part = part + sq[:, k:k + LANES]
    return jnp.sum(part.T, axis=0, keepdims=True)


def combine(parts):
    top = jnp.max(parts, axis=0, keepdims=True)
    return top + jnp.log2(jnp.sum(jnp.exp2(parts - top), axis=0, keepdims=True))


def repeat_kernel(a_ref, out_ref):
    for d in range(out_ref.shape[0]):
        out_ref[d] = a_ref[...]


def prepare_kernel(eps, a_ref, left_ref, a2_ref):
    x = a_ref[...]
    a2_ref[...] = row_norms(x) * (LOG2E / eps)
    hi, lo = split(x * (2.0 * LOG2E / eps))
    left_ref[...] = jnp.concatenate([hi, hi, lo], axis=1)


def pieces_kernel(eps, places, *refs):
    pieces, (bhi_ref, blo_ref, b2_ref) = refs[:len(places)], refs[-3:]
    me = lax.axis_index("aa")
    for ref, place in zip(pieces, places):
        y = ref[...]
        at = pl.ds(pl.multiple_of(place(me), y.shape[0]), y.shape[0])
        b2_ref[:, at] = row_norms(y) * (LOG2E / eps)
        bhi_ref[at, :], blo_ref[at, :] = split(y)


def scores_kernel(n, left, bhi_ref, blo_ref, b2_ref, s_ref, out_ref, top_ref, tot_ref):
    for start in range(0, s_ref.shape[1], n):
        at = pl.ds(start, n)
        hi, lo = bhi_ref[at, :], blo_ref[at, :]
        right = jnp.concatenate([hi, lo, hi], axis=1)
        x = lax.dot_general(left[...], right, (((1,), (1,)), ((), ())), preferred_element_type=jnp.float32)
        s_ref[:, at] = x
        x = x - b2_ref[:, at]
        parts = [x[:, k:k + LANES] for k in range(0, n, LANES)]
        top = tree(jnp.maximum, parts)
        if start == 0:
            tot_ref[...] = tree(jnp.add, [jnp.exp2(v - top) for v in parts])
        else:
            old = top_ref[...]
            top = jnp.maximum(old, top)
            tot_ref[...] = tot_ref[...] * jnp.exp2(old - top) + tree(jnp.add, [jnp.exp2(v - top) for v in parts])
        top_ref[...] = top
    finish_rows(top_ref, tot_ref, out_ref)


def finish_rows(top_ref, tot_ref, out_ref):
    m = top_ref[...].T
    peak = jnp.max(m, axis=0, keepdims=True)
    total = jnp.sum(tot_ref[...].T * jnp.exp2(m - peak), axis=0, keepdims=True)
    out_ref[...] = jnp.broadcast_to(peak + jnp.log2(total), out_ref.shape)


def row_pass_kernel(log_a, part_ref, s_ref, out_ref, wide, top, tot):
    wide[...] = jnp.broadcast_to(-combine(part_ref[...]) - log_a, wide.shape)
    cols = s_ref.shape[1] // LANES

    def group(r, carry):
        rows = pl.ds(pl.multiple_of(r * 8, 8), 8)
        m, l = None, None
        for half in range(0, cols, 16):
            x = [s_ref[rows, k * LANES:(k + 1) * LANES] + wide[:, k * LANES:(k + 1) * LANES]
                 for k in range(half, min(cols, half + 16))]
            m, l = online(m, l, x)
        top[rows, :] = m
        tot[rows, :] = l
        return carry

    lax.fori_loop(0, s_ref.shape[0] // 8, group, 0, unroll=16)
    finish_rows(top, tot, out_ref)


def online(m, l, x):
    top = tree(jnp.maximum, x)
    if m is None:
        return top, tree(jnp.add, [jnp.exp2(v - top) for v in x])
    new = jnp.maximum(m, top)
    return new, l * jnp.exp2(m - new) + tree(jnp.add, [jnp.exp2(v - new) for v in x])


def tree(op, xs):
    xs = list(xs)
    while len(xs) > 1:
        xs = [op(xs[i], xs[i + 1]) if i + 1 < len(xs) else xs[i] for i in range(0, len(xs), 2)]
    return xs[0]


def col_pass_kernel(log_b, eps, part_ref, a2_ref, s_ref, out_ref, alpha_ref, pot_ref, wide):
    alpha = -combine(part_ref[...]) - log_b
    alpha_ref[...] = alpha
    pot_ref[...] = (alpha + a2_ref[...]) * (eps / LOG2E)
    wide[...] = jnp.broadcast_to(alpha, (LANES, alpha.shape[1])).T
    rows = s_ref.shape[0]
    piece, across = 64, 8
    for start in range(0, s_ref.shape[1], LANES * across):
        cols = [slice(k, k + LANES) for k in range(start, start + LANES * across, LANES)]
        m, l = [None] * across, [None] * across
        for r in range(0, rows, piece):
            shift = [wide[q:q + 8, :] for q in range(r, r + piece, 8)]
            for k in range(across):
                x = [s_ref[q:q + 8, cols[k]] + shift[(q - r) // 8] for q in range(r, r + piece, 8)]
                m[k], l[k] = online(m[k], l[k], x)
        for k in range(across):
            peak = jnp.max(m[k], axis=0, keepdims=True)
            total = jnp.sum(l[k] * jnp.exp2(m[k] - peak), axis=0, keepdims=True)
            out_ref[:, cols[k]] = jnp.broadcast_to(peak + jnp.log2(total), (out_ref.shape[0], LANES))


def weights_kernel(log_a, log_b, eps, part_ref, alpha_ref, b2_ref, awide_ref, bwide_ref, pot_ref):
    beta = -combine(part_ref[...]) - log_a
    pot_ref[...] = (beta + b2_ref[...]) * (eps / LOG2E)
    bwide_ref[...] = jnp.broadcast_to(beta + log_b, bwide_ref.shape)
    awide_ref[...] = jnp.broadcast_to(alpha_ref[...], (LANES, alpha_ref.shape[1])).T


def grad_kernel(first, awide_ref, bwide_ref, a_ref, bhi_ref, blo_ref, s_ref, g_ref, mass):
    n = g_ref.shape[0]
    rows = pl.ds(pl.multiple_of(first(), n), n)
    step = 1024

    for start in range(0, s_ref.shape[1], step):
        at = pl.ds(start, step)
        hi_b, lo_b = bhi_ref[at, :], blo_ref[at, :]
        right = jnp.concatenate([hi_b, lo_b, hi_b], axis=0)
        alpha = awide_ref[rows, :]
        p = jnp.exp2(s_ref[rows, at] + jnp.concatenate([alpha] * (step // LANES), axis=1) + bwide_ref[:, at][:1, :])
        part = tree(jnp.add, [p[:, q:q + LANES] for q in range(0, step, LANES)])
        hi, lo = split(p)
        left = jnp.concatenate([hi, hi, lo], axis=1)
        pulled = jnp.dot(left, right, preferred_element_type=jnp.float32)
        mass[...] = part if start == 0 else mass[...] + part
        g_ref[...] = pulled if start == 0 else g_ref[...] + pulled
    g_ref[...] = 2.0 * (a_ref[rows, :] * jnp.sum(mass[...], axis=1, keepdims=True) - g_ref[...])


def turn_sum_kernel(order, *refs):
    parts, outs = refs[:2], refs[2:]
    n = outs[0].shape[0]
    for out_ref, first in zip(outs, order()):
        rows = pl.ds(pl.multiple_of(first * n, n), n)
        out_ref[...] = tree(jnp.add, [part[rows, :] for part in parts])


def sum_kernel(*refs):
    refs[-1][...] = tree(jnp.add, [part[...] for part in refs[:-1]])


VM = pl.BlockSpec(memory_space=pltpu.VMEM)


def call(kernel, outs, scratch, *args, limit=6 * MIB, cost=None):
    return pl.pallas_call(
        kernel,
        out_shape=outs,
        in_specs=[VM] * len(args),
        out_specs=[VM] * len(outs),
        scratch_shapes=scratch,
        cost_estimate=cost,
        compiler_params=pltpu.CompilerParams(vmem_limit_bytes=limit),
    )(*args)


def f32(*shape):
    return jax.ShapeDtypeStruct(shape, jnp.float32)


def v16(*shape):
    return pltpu.VMEM(shape, jnp.bfloat16)


def v32(*shape):
    return pltpu.VMEM(shape, jnp.float32)


def spread(x, axis):
    return lax.all_to_all(x, axis, 0, 0, tiled=True)


def body(points_a, points_b):
    na, nb = lax.axis_size("aa"), lax.axis_size("ba")
    share, width = points_a.shape
    piece = points_b.shape[0]
    rows_a, rows_b = share * nb, piece * na
    eps = width / 8.0
    log_a = -math.log2(rows_a * na)
    log_b = -math.log2(rows_b * nb)

    def move(x, by):
        return lax.ppermute(x, "aa", [(i, (i + 2 * by) % na) for i in range(na)])

    def swap(x):
        return lax.ppermute(x, "aa", [(i, i ^ 1) for i in range(na)])

    def place(by, flip, start=0):
        return lambda me: lax.rem(lax.bitwise_xor(me, flip) + 2 * by, na) * piece + start

    half = piece // 2
    up, down = move(points_b, 1), move(points_b, -1)
    low, high = move(up[:half], 1), move(down[half:], -1)
    wide, = call(repeat_kernel, [v32(nb, share, width)], [], points_a)
    whole_a = spread(wide, "ba").reshape(rows_a, width)
    pieces = [
        (points_b, place(0, 0)), (up, place(3, 0)), (down, place(1, 0)), (low, place(2, 0)), (high, place(2, 0, half)),
        (swap(points_b), place(0, 1)), (swap(up), place(3, 1)), (swap(down), place(1, 1)),
        (swap(low), place(2, 1)), (swap(high), place(2, 1, half))]
    bhi, blo, b2 = call(
        lambda *r: pieces_kernel(eps, [p for x, p in pieces], *r),
        [v16(rows_b, width), v16(rows_b, width), v32(1, rows_b)], [], *[x for x, p in pieces],
        cost=pl.CostEstimate(flops=0, bytes_accessed=64 * MIB, transcendentals=0))
    left, a2 = call(lambda *r: prepare_kernel(eps, *r), [v16(rows_a, 3 * width), v32(1, rows_a)], [], whole_a)
    s, rows = call(
        lambda *r: scores_kernel(piece, *r),
        [v32(rows_a, rows_b), v32(nb, rows_a)], [v32(rows_a, LANES), v32(rows_a, LANES)],
        left, bhi, blo, b2, limit=8 * MIB)
    for turn in range(ITERS):
        if turn > 0:
            rows, = call(
                lambda *r: row_pass_kernel(log_a, *r),
                [f32(nb, rows_a)],
                [v32(8, rows_b), v32(rows_a, LANES), v32(rows_a, LANES)],
                part, s)
        cols, alpha, pot_a = call(
            lambda *r: col_pass_kernel(log_b, eps, *r),
            [f32(na, rows_b), v32(1, rows_a), f32(1, rows_a)],
            [v32(rows_a, LANES)],
            spread(rows, "ba"), a2, s)
        part = spread(cols, "aa")
    awide, bwide, pot_b = call(
        lambda *r: weights_kernel(log_a, log_b, eps, *r),
        [v32(rows_a, LANES), v32(8, rows_b), f32(1, rows_b)], [], part, alpha, b2)

    def along_x(v, by):
        return lax.ppermute(v, "ba", [(i, (i + side * by) % nb) for i in range(nb)])

    def along_y(v, by):
        return lax.ppermute(v, "ba", [(i, i // side * side + (i + by) % side) for i in range(nb)])

    side = math.isqrt(nb)
    step = pl.CostEstimate(flops=2 * rows_a // side * width * rows_b, bytes_accessed=MIB, transcendentals=0)
    held = []
    for by in [2, 1, 3, 0]:
        g, = call(
            lambda *r: grad_kernel(lambda: lax.rem(lax.axis_index("ba") // side + by, side) * (rows_a // side), *r),
            [v32(rows_a // side, width)], [v32(rows_a // side, LANES)],
            awide, bwide, whole_a, bhi, blo, s, limit=12 * MIB, cost=step)
        held.append(along_x(g, by) if by else g)
    *arrived, total = held
    long = pl.CostEstimate(flops=9 * step.flops, bytes_accessed=4 * MIB, transcendentals=0)
    for g in arrived[:-1]:
        total, = call(sum_kernel, [v32(rows_a // side, width)], [], total, g, cost=long)
    cuts = call(
        lambda *r: turn_sum_kernel(lambda: [lax.rem(lax.rem(lax.axis_index("ba"), side) + by, side) for by in range(side)], *r),
        [v32(share, width)] * side, [], total, arrived[-1])
    grad, = call(sum_kernel, [f32(share, width)], [], cuts[0], *[along_y(cuts[by], by) for by in (2, 1, 3)])
    return (pot_a.reshape(rows_a), pot_b.reshape(rows_b), grad)


def solution(mesh):
    placed = (P(("aa", "ba"), None), P(("ba", "aa"), None))
    return jax.shard_map(
        body,
        mesh=mesh,
        in_specs=placed,
        out_specs=(P("aa"), P("ba"), P(("aa", "ba"), None)),
        check_vma=False,
    )
```

```python
import math

import jax
import jax.numpy as jnp
from jax import lax
from jax.experimental import pallas as pl
from jax.experimental.pallas import tpu as pltpu
from jax.sharding import PartitionSpec as P

ITERS = 2
LOG2E = math.log2(math.e)
LANES = 128
MIB = 1024 * 1024


def split(x):
    hi = x.astype(jnp.bfloat16)
    return hi, (x - hi.astype(jnp.float32)).astype(jnp.bfloat16)


def row_norms(x):
    sq = x * x
    part = sq[:, :LANES]
    for k in range(LANES, sq.shape[1], LANES):
        part = part + sq[:, k:k + LANES]
    return jnp.sum(part.T, axis=0, keepdims=True)


def combine(parts):
    top = jnp.max(parts, axis=0, keepdims=True)
    return top + jnp.log2(jnp.sum(jnp.exp2(parts - top), axis=0, keepdims=True))


def repeat_kernel(a_ref, out_ref):
    for d in range(out_ref.shape[0]):
        out_ref[d] = a_ref[...]


def pieces_kernel(eps, places, a_ref, *refs):
    pieces, (left_ref, a2_ref, bhi_ref, blo_ref, b2_ref, held, sems) = refs[:len(places)], refs[len(places):]
    spots, at = [], 0
    for ref in pieces:
        spots.append(pl.ds(at, ref.shape[0]))
        at += ref.shape[0]
    loads = [pltpu.make_async_copy(ref, held.at[spot], sems.at[k]) for k, (ref, spot) in enumerate(zip(pieces, spots))]
    for load in loads:
        load.start()
    x = a_ref[...]
    a2_ref[...] = row_norms(x) * (LOG2E / eps)
    hi, lo = split(x * (2.0 * LOG2E / eps))
    left_ref[...] = jnp.concatenate([hi, hi, lo], axis=1)
    me = lax.axis_index("aa")
    for load, spot, place in zip(loads, spots, places):
        load.wait()
        y = held[spot, :]
        to = pl.ds(pl.multiple_of(place(me), spot.size), spot.size)
        b2_ref[:, to] = row_norms(y) * (LOG2E / eps)
        bhi_ref[to, :], blo_ref[to, :] = split(y)


def scores_kernel(n, left, bhi_ref, blo_ref, b2_ref, s_ref, out_ref, top_ref, tot_ref):
    for start in range(0, s_ref.shape[1], n):
        at = pl.ds(start, n)
        hi, lo = bhi_ref[at, :], blo_ref[at, :]
        right = jnp.concatenate([hi, lo, hi], axis=1)
        x = lax.dot_general(left[...], right, (((1,), (1,)), ((), ())), preferred_element_type=jnp.float32)
        s_ref[:, at] = x
        x = x - b2_ref[:, at]
        parts = [x[:, k:k + LANES] for k in range(0, n, LANES)]
        top = tree(jnp.maximum, parts)
        if start == 0:
            tot_ref[...] = tree(jnp.add, [jnp.exp2(v - top) for v in parts])
        else:
            old = top_ref[...]
            top = jnp.maximum(old, top)
            tot_ref[...] = tot_ref[...] * jnp.exp2(old - top) + tree(jnp.add, [jnp.exp2(v - top) for v in parts])
        top_ref[...] = top
    finish_rows(top_ref, tot_ref, out_ref)


def finish_rows(top_ref, tot_ref, out_ref):
    m = top_ref[...].T
    peak = jnp.max(m, axis=0, keepdims=True)
    total = jnp.sum(tot_ref[...].T * jnp.exp2(m - peak), axis=0, keepdims=True)
    out_ref[...] = jnp.broadcast_to(peak + jnp.log2(total), out_ref.shape)


def row_pass_kernel(log_a, part_ref, s_ref, out_ref, wide, top, tot):
    wide[...] = jnp.broadcast_to(-combine(part_ref[...]) - log_a, wide.shape)
    cols = s_ref.shape[1] // LANES

    def group(r, carry):
        rows = pl.ds(pl.multiple_of(r * 8, 8), 8)
        m, l = None, None
        for half in range(0, cols, 16):
            x = [s_ref[rows, k * LANES:(k + 1) * LANES] + wide[:, k * LANES:(k + 1) * LANES]
                 for k in range(half, min(cols, half + 16))]
            m, l = online(m, l, x)
        top[rows, :] = m
        tot[rows, :] = l
        return carry

    lax.fori_loop(0, s_ref.shape[0] // 8, group, 0, unroll=16)
    finish_rows(top, tot, out_ref)


def online(m, l, x):
    top = tree(jnp.maximum, x)
    if m is None:
        return top, tree(jnp.add, [jnp.exp2(v - top) for v in x])
    new = jnp.maximum(m, top)
    return new, l * jnp.exp2(m - new) + tree(jnp.add, [jnp.exp2(v - new) for v in x])


def tree(op, xs):
    xs = list(xs)
    while len(xs) > 1:
        xs = [op(xs[i], xs[i + 1]) if i + 1 < len(xs) else xs[i] for i in range(0, len(xs), 2)]
    return xs[0]


def col_pass_kernel(log_b, eps, part_ref, a2_ref, s_ref, out_ref, wide, pot_ref):
    alpha = -combine(part_ref[...]) - log_b
    pot_ref[...] = (alpha + a2_ref[...]) * (eps / LOG2E)
    wide[...] = jnp.broadcast_to(alpha, (LANES, alpha.shape[1])).T
    rows = s_ref.shape[0]
    piece, across = 64, 8
    for start in range(0, s_ref.shape[1], LANES * across):
        cols = [slice(k, k + LANES) for k in range(start, start + LANES * across, LANES)]
        m, l = [None] * across, [None] * across
        for r in range(0, rows, piece):
            shift = [wide[q:q + 8, :] for q in range(r, r + piece, 8)]
            for k in range(across):
                x = [s_ref[q:q + 8, cols[k]] + shift[(q - r) // 8] for q in range(r, r + piece, 8)]
                m[k], l[k] = online(m[k], l[k], x)
        for k in range(across):
            peak = jnp.max(m[k], axis=0, keepdims=True)
            total = jnp.sum(l[k] * jnp.exp2(m[k] - peak), axis=0, keepdims=True)
            out_ref[:, cols[k]] = jnp.broadcast_to(peak + jnp.log2(total), (out_ref.shape[0], LANES))


def grad_kernel(first, awide_ref, bwide_ref, a_ref, bhi_ref, blo_ref, s_ref, g_ref, mass):
    n = g_ref.shape[0]
    rows = pl.ds(pl.multiple_of(first(), n), n)
    step = 1024

    for start in range(0, s_ref.shape[1], step):
        at = pl.ds(start, step)
        hi_b, lo_b = bhi_ref[at, :], blo_ref[at, :]
        right = jnp.concatenate([hi_b, lo_b, hi_b], axis=0)
        alpha = awide_ref[rows, :]
        p = jnp.exp2(s_ref[rows, at] + jnp.concatenate([alpha] * (step // LANES), axis=1) + bwide_ref[:, at][:1, :])
        part = tree(jnp.add, [p[:, q:q + LANES] for q in range(0, step, LANES)])
        hi, lo = split(p)
        left = jnp.concatenate([hi, hi, lo], axis=1)
        pulled = jnp.dot(left, right, preferred_element_type=jnp.float32)
        mass[...] = part if start == 0 else mass[...] + part
        g_ref[...] = pulled if start == 0 else g_ref[...] + pulled
    g_ref[...] = 2.0 * (a_ref[rows, :] * jnp.sum(mass[...], axis=1, keepdims=True) - g_ref[...])


def first_grad_kernel(log_a, log_b, eps, first, part_ref, b2_ref, awide_ref, a_ref, bhi_ref, blo_ref, s_ref,
                      bwide_ref, pot_ref, g_ref, mass):
    beta = -combine(part_ref[...]) - log_a
    pot_ref[...] = (beta + b2_ref[...]) * (eps / LOG2E)
    bwide_ref[...] = jnp.broadcast_to(beta + log_b, bwide_ref.shape)
    grad_kernel(first, awide_ref, bwide_ref, a_ref, bhi_ref, blo_ref, s_ref, g_ref, mass)


def turn_sum_kernel(order, *refs):
    parts, outs = refs[:2], refs[2:]
    n = outs[0].shape[0]
    for out_ref, first in zip(outs, order()):
        rows = pl.ds(pl.multiple_of(first * n, n), n)
        out_ref[...] = tree(jnp.add, [part[rows, :] for part in parts])


def sum_kernel(*refs):
    refs[-1][...] = tree(jnp.add, [part[...] for part in refs[:-1]])


VM = pl.BlockSpec(memory_space=pltpu.VMEM)


def call(kernel, outs, scratch, *args, limit=6 * MIB, cost=None, ins=None):
    return pl.pallas_call(
        kernel,
        out_shape=outs,
        in_specs=ins or [VM] * len(args),
        out_specs=[VM] * len(outs),
        scratch_shapes=scratch,
        cost_estimate=cost,
        compiler_params=pltpu.CompilerParams(vmem_limit_bytes=limit),
    )(*args)


def f32(*shape):
    return jax.ShapeDtypeStruct(shape, jnp.float32)


def v16(*shape):
    return pltpu.VMEM(shape, jnp.bfloat16)


def v32(*shape):
    return pltpu.VMEM(shape, jnp.float32)


def spread(x, axis):
    return lax.all_to_all(x, axis, 0, 0, tiled=True)


def body(points_a, points_b):
    na, nb = lax.axis_size("aa"), lax.axis_size("ba")
    share, width = points_a.shape
    piece = points_b.shape[0]
    rows_a, rows_b = share * nb, piece * na
    eps = width / 8.0
    log_a = -math.log2(rows_a * na)
    log_b = -math.log2(rows_b * nb)

    def move(x, by):
        return lax.ppermute(x, "aa", [(i, (i + 2 * by) % na) for i in range(na)])

    def swap(x):
        return lax.ppermute(x, "aa", [(i, i ^ 1) for i in range(na)])

    def place(by, flip, start=0):
        return lambda me: lax.rem(lax.bitwise_xor(me, flip) + 2 * by, na) * piece + start

    half = piece // 2
    up, down = move(points_b, 1), move(points_b, -1)
    low, high = move(up[:half], 1), move(down[half:], -1)
    wide, = call(repeat_kernel, [v32(nb, share, width)], [], points_a)
    whole_a = spread(wide, "ba").reshape(rows_a, width)
    pieces = [
        (points_b, place(0, 0)), (up, place(3, 0)), (down, place(1, 0)), (low, place(2, 0)), (high, place(2, 0, half)),
        (swap(points_b), place(0, 1)), (swap(up), place(3, 1)), (swap(down), place(1, 1)),
        (swap(low), place(2, 1)), (swap(high), place(2, 1, half))]
    left, a2, bhi, blo, b2 = call(
        lambda *r: pieces_kernel(eps, [p for x, p in pieces], *r),
        [v16(rows_a, 3 * width), v32(1, rows_a), v16(rows_b, width), v16(rows_b, width), v32(1, rows_b)],
        [v32(rows_b, width), pltpu.SemaphoreType.DMA((len(pieces),))],
        whole_a, *[x for x, p in pieces], limit=12 * MIB,
        ins=[VM] + [pl.BlockSpec(memory_space=pl.ANY)] * len(pieces))
    s, rows = call(
        lambda *r: scores_kernel(piece, *r),
        [v32(rows_a, rows_b), v32(nb, rows_a)], [v32(rows_a, LANES), v32(rows_a, LANES)],
        left, bhi, blo, b2, limit=8 * MIB)
    for turn in range(ITERS):
        if turn > 0:
            rows, = call(
                lambda *r: row_pass_kernel(log_a, *r),
                [f32(nb, rows_a)],
                [v32(8, rows_b), v32(rows_a, LANES), v32(rows_a, LANES)],
                part, s)
        cols, awide, pot_a = call(
            lambda *r: col_pass_kernel(log_b, eps, *r),
            [f32(na, rows_b), v32(rows_a, LANES), f32(1, rows_a)], [],
            spread(rows, "ba"), a2, s)
        part = spread(cols, "aa")
    def along_x(v, by):
        return lax.ppermute(v, "ba", [(i, (i + side * by) % nb) for i in range(nb)])

    def along_y(v, by):
        return lax.ppermute(v, "ba", [(i, i // side * side + (i + by) % side) for i in range(nb)])

    side = math.isqrt(nb)
    step = pl.CostEstimate(flops=2 * rows_a // side * width * rows_b, bytes_accessed=MIB, transcendentals=0)
    held = []
    group = rows_a // side
    shared = awide, whole_a, bhi, blo, s
    for by in [2, 1, 3, 0]:
        def first():
            return lax.rem(lax.axis_index("ba") // side + by, side) * group

        if not held:
            bwide, pot_b, g = call(
                lambda *r: first_grad_kernel(log_a, log_b, eps, first, *r),
                [v32(8, rows_b), f32(1, rows_b), v32(group, width)], [v32(group, LANES)],
                part, b2, *shared, limit=12 * MIB, cost=step)
        else:
            g, = call(
                lambda awide, a, bhi, blo, s, bwide, *r: grad_kernel(first, awide, bwide, a, bhi, blo, s, *r),
                [v32(group, width)], [v32(group, LANES)],
                *shared, bwide, limit=12 * MIB, cost=step)
        held.append(along_x(g, by) if by else g)
    *arrived, total = held
    long = pl.CostEstimate(flops=9 * step.flops, bytes_accessed=4 * MIB, transcendentals=0)
    for g in arrived[:-1]:
        total, = call(sum_kernel, [v32(rows_a // side, width)], [], total, g, cost=long)
    cuts = call(
        lambda *r: turn_sum_kernel(lambda: [lax.rem(lax.rem(lax.axis_index("ba"), side) + by, side) for by in range(side)], *r),
        [v32(share, width)] * side, [], total, arrived[-1])
    grad, = call(sum_kernel, [f32(share, width)], [], cuts[0], *[along_y(cuts[by], by) for by in (2, 1, 3)])
    return (pot_a.reshape(rows_a), pot_b.reshape(rows_b), grad)


def solution(mesh):
    placed = (P(("aa", "ba"), None), P(("ba", "aa"), None))
    return jax.shard_map(
        body,
        mesh=mesh,
        in_specs=placed,
        out_specs=(P("aa"), P("ba"), P(("aa", "ba"), None)),
        check_vma=False,
    )
```

```python
import math

import jax
import jax.numpy as jnp
from jax import lax
from jax.experimental import pallas as pl
from jax.experimental.pallas import tpu as pltpu
from jax.sharding import PartitionSpec as P

ITERS = 2
LOG2E = math.log2(math.e)
LANES = 128
MIB = 1024 * 1024


def split(x):
    hi = x.astype(jnp.bfloat16)
    return hi, (x - hi.astype(jnp.float32)).astype(jnp.bfloat16)


def row_norms(x):
    sq = x * x
    part = sq[:, :LANES]
    for k in range(LANES, sq.shape[1], LANES):
        part = part + sq[:, k:k + LANES]
    return jnp.sum(part.T, axis=0, keepdims=True)


def combine(parts):
    top = jnp.max(parts, axis=0, keepdims=True)
    return top + jnp.log2(jnp.sum(jnp.exp2(parts - top), axis=0, keepdims=True))


def repeat_kernel(a_ref, out_ref):
    for d in range(out_ref.shape[0]):
        out_ref[d] = a_ref[...]


def pieces_kernel(eps, places, a_ref, *refs):
    pieces, (left_ref, a2_ref, bhi_ref, blo_ref, b2_ref, held, sems) = refs[:len(places)], refs[len(places):]
    spots, at = [], 0
    for ref in pieces:
        spots.append(pl.ds(at, ref.shape[0]))
        at += ref.shape[0]
    loads = [pltpu.make_async_copy(ref, held.at[spot], sems.at[k]) for k, (ref, spot) in enumerate(zip(pieces, spots))]
    for load in loads:
        load.start()
    x = a_ref[...]
    a2_ref[...] = row_norms(x) * (LOG2E / eps)
    hi, lo = split(x * (2.0 * LOG2E / eps))
    left_ref[...] = jnp.concatenate([hi, hi, lo], axis=1)
    me = lax.axis_index("aa")
    for load, spot, place in zip(loads, spots, places):
        load.wait()
        y = held[spot, :]
        to = pl.ds(pl.multiple_of(place(me), spot.size), spot.size)
        b2_ref[:, to] = row_norms(y) * (LOG2E / eps)
        bhi_ref[to, :], blo_ref[to, :] = split(y)


def scores_kernel(n, left, bhi_ref, blo_ref, b2_ref, s_ref, out_ref, top_ref, tot_ref):
    for start in range(0, s_ref.shape[1], n):
        at = pl.ds(start, n)
        hi, lo = bhi_ref[at, :], blo_ref[at, :]
        right = jnp.concatenate([hi, lo, hi], axis=1)
        x = lax.dot_general(left[...], right, (((1,), (1,)), ((), ())), preferred_element_type=jnp.float32)
        s_ref[:, at] = x
        x = x - b2_ref[:, at]
        parts = [x[:, k:k + LANES] for k in range(0, n, LANES)]
        top = tree(jnp.maximum, parts)
        if start == 0:
            tot_ref[...] = tree(jnp.add, [jnp.exp2(v - top) for v in parts])
        else:
            old = top_ref[...]
            top = jnp.maximum(old, top)
            tot_ref[...] = tot_ref[...] * jnp.exp2(old - top) + tree(jnp.add, [jnp.exp2(v - top) for v in parts])
        top_ref[...] = top
    finish_rows(top_ref, tot_ref, out_ref)


def finish_rows(top_ref, tot_ref, out_ref):
    m = top_ref[...].T
    peak = jnp.max(m, axis=0, keepdims=True)
    total = jnp.sum(tot_ref[...].T * jnp.exp2(m - peak), axis=0, keepdims=True)
    out_ref[...] = jnp.broadcast_to(peak + jnp.log2(total), out_ref.shape)


def row_pass_kernel(log_a, part_ref, s_ref, out_ref, wide, top, tot):
    wide[...] = jnp.broadcast_to(-combine(part_ref[...]) - log_a, wide.shape)
    cols = s_ref.shape[1] // LANES

    def group(r, carry):
        rows = pl.ds(pl.multiple_of(r * 8, 8), 8)
        m, l = None, None
        for half in range(0, cols, 16):
            x = [s_ref[rows, k * LANES:(k + 1) * LANES] + wide[:, k * LANES:(k + 1) * LANES]
                 for k in range(half, min(cols, half + 16))]
            m, l = online(m, l, x)
        top[rows, :] = m
        tot[rows, :] = l
        return carry

    lax.fori_loop(0, s_ref.shape[0] // 8, group, 0, unroll=16)
    finish_rows(top, tot, out_ref)


def online(m, l, x):
    top = tree(jnp.maximum, x)
    if m is None:
        return top, tree(jnp.add, [jnp.exp2(v - top) for v in x])
    new = jnp.maximum(m, top)
    return new, l * jnp.exp2(m - new) + tree(jnp.add, [jnp.exp2(v - new) for v in x])


def tree(op, xs):
    xs = list(xs)
    while len(xs) > 1:
        xs = [op(xs[i], xs[i + 1]) if i + 1 < len(xs) else xs[i] for i in range(0, len(xs), 2)]
    return xs[0]


def col_pass_kernel(log_b, eps, part_ref, a2_ref, s_ref, out_ref, pot_ref, wide):
    alpha = -combine(part_ref[...]) - log_b
    pot_ref[...] = (alpha + a2_ref[...]) * (eps / LOG2E)
    wide[...] = jnp.broadcast_to(alpha, (LANES, alpha.shape[1])).T
    rows = s_ref.shape[0]
    piece, across = 64, 8
    for start in range(0, s_ref.shape[1], LANES * across):
        cols = [slice(k, k + LANES) for k in range(start, start + LANES * across, LANES)]
        m, l = [None] * across, [None] * across
        for r in range(0, rows, piece):
            shift = [wide[q:q + 8, :] for q in range(r, r + piece, 8)]
            for k in range(across):
                x = [s_ref[q:q + 8, cols[k]] + shift[(q - r) // 8] for q in range(r, r + piece, 8)]
                m[k], l[k] = online(m[k], l[k], x)
        for k in range(across):
            peak = jnp.max(m[k], axis=0, keepdims=True)
            total = jnp.sum(l[k] * jnp.exp2(m[k] - peak), axis=0, keepdims=True)
            out_ref[:, cols[k]] = jnp.broadcast_to(peak + jnp.log2(total), (out_ref.shape[0], LANES))


def grad_kernel(first, awide_ref, bwide_ref, a_ref, bhi_ref, blo_ref, s_ref, g_ref, mass):
    n = g_ref.shape[0]
    rows = pl.ds(pl.multiple_of(first(), n), n)
    step = 1024

    for start in range(0, s_ref.shape[1], step):
        at = pl.ds(start, step)
        hi_b, lo_b = bhi_ref[at, :], blo_ref[at, :]
        right = jnp.concatenate([hi_b, lo_b, hi_b], axis=0)
        alpha = awide_ref[rows, :]
        p = jnp.exp2(s_ref[rows, at] + jnp.concatenate([alpha] * (step // LANES), axis=1) + bwide_ref[:, at][:1, :])
        part = tree(jnp.add, [p[:, q:q + LANES] for q in range(0, step, LANES)])
        hi, lo = split(p)
        left = jnp.concatenate([hi, hi, lo], axis=1)
        pulled = jnp.dot(left, right, preferred_element_type=jnp.float32)
        mass[...] = part if start == 0 else mass[...] + part
        g_ref[...] = pulled if start == 0 else g_ref[...] + pulled
    g_ref[...] = 2.0 * (a_ref[rows, :] * jnp.sum(mass[...], axis=1, keepdims=True) - g_ref[...])


def weights_kernel(log_a, log_b, eps, part_ref, b2_ref, bwide_ref, pot_ref):
    beta = -combine(part_ref[...]) - log_a
    pot_ref[...] = (beta + b2_ref[...]) * (eps / LOG2E)
    bwide_ref[...] = jnp.broadcast_to(beta + log_b, bwide_ref.shape)


def turn_sum_kernel(order, *refs):
    parts, outs = refs[:2], refs[2:]
    n = outs[0].shape[0]
    for out_ref, first in zip(outs, order()):
        rows = pl.ds(pl.multiple_of(first * n, n), n)
        out_ref[...] = tree(jnp.add, [part[rows, :] for part in parts])


def sum_kernel(*refs):
    refs[-1][...] = tree(jnp.add, [part[...] for part in refs[:-1]])


VM = pl.BlockSpec(memory_space=pltpu.VMEM)


def call(kernel, outs, scratch, *args, limit=6 * MIB, cost=None, ins=None):
    return pl.pallas_call(
        kernel,
        out_shape=outs,
        in_specs=ins or [VM] * len(args),
        out_specs=[VM] * len(outs),
        scratch_shapes=scratch,
        cost_estimate=cost,
        compiler_params=pltpu.CompilerParams(vmem_limit_bytes=limit),
    )(*args)


def f32(*shape):
    return jax.ShapeDtypeStruct(shape, jnp.float32)


def v16(*shape):
    return pltpu.VMEM(shape, jnp.bfloat16)


def v32(*shape):
    return pltpu.VMEM(shape, jnp.float32)


def spread(x, axis):
    return lax.all_to_all(x, axis, 0, 0, tiled=True)


def body(points_a, points_b):
    na, nb = lax.axis_size("aa"), lax.axis_size("ba")
    share, width = points_a.shape
    piece = points_b.shape[0]
    rows_a, rows_b = share * nb, piece * na
    eps = width / 8.0
    log_a = -math.log2(rows_a * na)
    log_b = -math.log2(rows_b * nb)

    def move(x, by):
        return lax.ppermute(x, "aa", [(i, (i + 2 * by) % na) for i in range(na)])

    def swap(x):
        return lax.ppermute(x, "aa", [(i, i ^ 1) for i in range(na)])

    def place(by, flip, start=0):
        return lambda me: lax.rem(lax.bitwise_xor(me, flip) + 2 * by, na) * piece + start

    half = piece // 2
    up, down = move(points_b, 1), move(points_b, -1)
    low, high = move(up[:half], 1), move(down[half:], -1)
    wide, = call(repeat_kernel, [v32(nb, share, width)], [], points_a)
    whole_a = spread(wide, "ba").reshape(rows_a, width)
    pieces = [
        (points_b, place(0, 0)), (up, place(3, 0)), (down, place(1, 0)), (low, place(2, 0)), (high, place(2, 0, half)),
        (swap(points_b), place(0, 1)), (swap(up), place(3, 1)), (swap(down), place(1, 1)),
        (swap(low), place(2, 1)), (swap(high), place(2, 1, half))]
    left, a2, bhi, blo, b2 = call(
        lambda *r: pieces_kernel(eps, [p for x, p in pieces], *r),
        [v16(rows_a, 3 * width), v32(1, rows_a), v16(rows_b, width), v16(rows_b, width), v32(1, rows_b)],
        [v32(rows_b, width), pltpu.SemaphoreType.DMA((len(pieces),))],
        whole_a, *[x for x, p in pieces], limit=12 * MIB,
        ins=[VM] + [pl.BlockSpec(memory_space=pl.ANY)] * len(pieces))
    s, rows = call(
        lambda *r: scores_kernel(piece, *r),
        [v32(rows_a, rows_b), v32(nb, rows_a)], [v32(rows_a, LANES), v32(rows_a, LANES)],
        left, bhi, blo, b2, limit=8 * MIB)
    for turn in range(ITERS):
        if turn > 0:
            rows, = call(
                lambda *r: row_pass_kernel(log_a, *r),
                [f32(nb, rows_a)],
                [v32(8, rows_b), v32(rows_a, LANES), v32(rows_a, LANES)],
                part, s)
        final = turn == ITERS - 1
        wide_shape = [v32(rows_a, LANES)]
        cols, pot_a, *awide = call(
            lambda *r: col_pass_kernel(log_b, eps, *r),
            [f32(na, rows_b), f32(1, rows_a)] + wide_shape * final, wide_shape * (not final),
            spread(rows, "ba"), a2, s)
        part = spread(cols, "aa")
    def along_x(v, by):
        return lax.ppermute(v, "ba", [(i, (i + side * by) % nb) for i in range(nb)])

    def along_y(v, by):
        return lax.ppermute(v, "ba", [(i, i // side * side + (i + by) % side) for i in range(nb)])

    side = math.isqrt(nb)
    step = pl.CostEstimate(flops=2 * rows_a // side * width * rows_b, bytes_accessed=MIB, transcendentals=0)
    held = []
    bwide, pot_b = call(
        lambda *r: weights_kernel(log_a, log_b, eps, *r), [v32(8, rows_b), f32(1, rows_b)], [], part, b2)
    for by in [2, 1, 3, 0]:
        g, = call(
            lambda *r: grad_kernel(lambda: lax.rem(lax.axis_index("ba") // side + by, side) * (rows_a // side), *r),
            [v32(rows_a // side, width)], [v32(rows_a // side, LANES)],
            *awide, bwide, whole_a, bhi, blo, s, limit=12 * MIB, cost=step)
        held.append(along_x(g, by) if by else g)
    *arrived, total = held
    long = pl.CostEstimate(flops=9 * step.flops, bytes_accessed=4 * MIB, transcendentals=0)
    for g in arrived[:-1]:
        total, = call(sum_kernel, [v32(rows_a // side, width)], [], total, g, cost=long)
    cuts = call(
        lambda *r: turn_sum_kernel(lambda: [lax.rem(lax.rem(lax.axis_index("ba"), side) + by, side) for by in range(side)], *r),
        [v32(share, width)] * side, [], total, arrived[-1])
    grad, = call(sum_kernel, [f32(share, width)], [], cuts[0], *[along_y(cuts[by], by) for by in (2, 1, 3)])
    return (pot_a.reshape(rows_a), pot_b.reshape(rows_b), grad)


def solution(mesh):
    placed = (P(("aa", "ba"), None), P(("ba", "aa"), None))
    return jax.shard_map(
        body,
        mesh=mesh,
        in_specs=placed,
        out_specs=(P("aa"), P("ba"), P(("aa", "ba"), None)),
        check_vma=False,
    )
```

```python
import math

import jax
import jax.numpy as jnp
from jax import lax
from jax.experimental import pallas as pl
from jax.experimental.pallas import tpu as pltpu
from jax.sharding import PartitionSpec as P

ITERS = 2
LOG2E = math.log2(math.e)
LANES = 128
MIB = 1024 * 1024


def split(x):
    hi = x.astype(jnp.bfloat16)
    return hi, (x - hi.astype(jnp.float32)).astype(jnp.bfloat16)


def row_norms(x):
    sq = x * x
    part = sq[:, :LANES]
    for k in range(LANES, sq.shape[1], LANES):
        part = part + sq[:, k:k + LANES]
    return jnp.sum(part.T, axis=0, keepdims=True)


def combine(parts):
    top = jnp.max(parts, axis=0, keepdims=True)
    return top + jnp.log2(jnp.sum(jnp.exp2(parts - top), axis=0, keepdims=True))


def repeat_kernel(a_ref, out_ref):
    for d in range(out_ref.shape[0]):
        out_ref[d] = a_ref[...]


def pieces_kernel(eps, places, a_ref, *refs):
    pieces, (left_ref, a2_ref, bhi_ref, blo_ref, b2_ref, held, sems) = refs[:len(places)], refs[len(places):]
    spots, at = [], 0
    for ref in pieces:
        spots.append(pl.ds(at, ref.shape[0]))
        at += ref.shape[0]
    loads = [pltpu.make_async_copy(ref, held.at[spot], sems.at[k]) for k, (ref, spot) in enumerate(zip(pieces, spots))]
    for load in loads:
        load.start()
    x = a_ref[...]
    a2_ref[...] = row_norms(x) * (LOG2E / eps)
    hi, lo = split(x * (2.0 * LOG2E / eps))
    left_ref[...] = jnp.concatenate([hi, hi, lo], axis=1)
    me = lax.axis_index("aa")
    for load, spot, place in zip(loads, spots, places):
        load.wait()
        y = held[spot, :]
        to = pl.ds(pl.multiple_of(place(me), spot.size), spot.size)
        b2_ref[:, to] = row_norms(y) * (LOG2E / eps)
        bhi_ref[to, :], blo_ref[to, :] = split(y)


def scores_kernel(n, left, bhi_ref, blo_ref, b2_ref, s_ref, out_ref, top_ref, tot_ref):
    for start in range(0, s_ref.shape[1], n):
        at = pl.ds(start, n)
        hi, lo = bhi_ref[at, :], blo_ref[at, :]
        right = jnp.concatenate([hi, lo, hi], axis=1)
        x = lax.dot_general(left[...], right, (((1,), (1,)), ((), ())), preferred_element_type=jnp.float32)
        s_ref[:, at] = x
        x = x - b2_ref[:, at]
        parts = [x[:, k:k + LANES] for k in range(0, n, LANES)]
        top = tree(jnp.maximum, parts)
        if start == 0:
            tot_ref[...] = tree(jnp.add, [jnp.exp2(v - top) for v in parts])
        else:
            old = top_ref[...]
            top = jnp.maximum(old, top)
            tot_ref[...] = tot_ref[...] * jnp.exp2(old - top) + tree(jnp.add, [jnp.exp2(v - top) for v in parts])
        top_ref[...] = top
    finish_rows(top_ref, tot_ref, out_ref)


def finish_rows(top_ref, tot_ref, out_ref):
    m = top_ref[...].T
    peak = jnp.max(m, axis=0, keepdims=True)
    total = jnp.sum(tot_ref[...].T * jnp.exp2(m - peak), axis=0, keepdims=True)
    out_ref[...] = jnp.broadcast_to(peak + jnp.log2(total), out_ref.shape)


def row_pass_kernel(log_a, part_ref, s_ref, out_ref, wide, top, tot):
    wide[...] = jnp.broadcast_to(-combine(part_ref[...]) - log_a, wide.shape)
    cols = s_ref.shape[1] // LANES

    def group(r, carry):
        rows = pl.ds(pl.multiple_of(r * 8, 8), 8)
        m, l = None, None
        for half in range(0, cols, 16):
            x = [s_ref[rows, k * LANES:(k + 1) * LANES] + wide[:, k * LANES:(k + 1) * LANES]
                 for k in range(half, min(cols, half + 16))]
            m, l = online(m, l, x)
        top[rows, :] = m
        tot[rows, :] = l
        return carry

    lax.fori_loop(0, s_ref.shape[0] // 8, group, 0, unroll=16)
    finish_rows(top, tot, out_ref)


def online(m, l, x):
    top = tree(jnp.maximum, x)
    if m is None:
        return top, tree(jnp.add, [jnp.exp2(v - top) for v in x])
    new = jnp.maximum(m, top)
    return new, l * jnp.exp2(m - new) + tree(jnp.add, [jnp.exp2(v - new) for v in x])


def tree(op, xs):
    xs = list(xs)
    while len(xs) > 1:
        xs = [op(xs[i], xs[i + 1]) if i + 1 < len(xs) else xs[i] for i in range(0, len(xs), 2)]
    return xs[0]


def col_pass_kernel(log_b, eps, part_ref, a2_ref, s_ref, out_ref, pot_ref, wide):
    alpha = -combine(part_ref[...]) - log_b
    pot_ref[...] = (alpha + a2_ref[...]) * (eps / LOG2E)
    wide[...] = jnp.broadcast_to(alpha, (LANES, alpha.shape[1])).T
    rows = s_ref.shape[0]
    piece, across = 64, 8
    for start in range(0, s_ref.shape[1], LANES * across):
        cols = [slice(k, k + LANES) for k in range(start, start + LANES * across, LANES)]
        m, l = [None] * across, [None] * across
        for r in range(0, rows, piece):
            shift = [wide[q:q + 8, :] for q in range(r, r + piece, 8)]
            for k in range(across):
                x = [s_ref[q:q + 8, cols[k]] + shift[(q - r) // 8] for q in range(r, r + piece, 8)]
                m[k], l[k] = online(m[k], l[k], x)
        for k in range(across):
            peak = jnp.max(m[k], axis=0, keepdims=True)
            total = jnp.sum(l[k] * jnp.exp2(m[k] - peak), axis=0, keepdims=True)
            out_ref[:, cols[k]] = jnp.broadcast_to(peak + jnp.log2(total), (out_ref.shape[0], LANES))


def grad_kernel(first, awide_ref, bwide_ref, a_ref, bhi_ref, blo_ref, s_ref, g_ref, mass):
    n = g_ref.shape[0]
    rows = pl.ds(pl.multiple_of(first(), n), n)
    step = 256

    for start in range(0, s_ref.shape[1], step):
        at = pl.ds(start, step)
        hi_b, lo_b = bhi_ref[at, :], blo_ref[at, :]
        right = jnp.concatenate([hi_b, lo_b, hi_b], axis=0)
        alpha = awide_ref[rows, :]
        p = jnp.exp2(s_ref[rows, at] + jnp.concatenate([alpha] * (step // LANES), axis=1) + bwide_ref[:, at][:1, :])
        part = tree(jnp.add, [p[:, q:q + LANES] for q in range(0, step, LANES)])
        hi, lo = split(p)
        left = jnp.concatenate([hi, hi, lo], axis=1)
        pulled = jnp.dot(left, right, preferred_element_type=jnp.float32)
        mass[...] = part if start == 0 else mass[...] + part
        g_ref[...] = pulled if start == 0 else g_ref[...] + pulled
    g_ref[...] = 2.0 * (a_ref[rows, :] * jnp.sum(mass[...], axis=1, keepdims=True) - g_ref[...])


def weights_kernel(log_a, log_b, eps, part_ref, b2_ref, bwide_ref, pot_ref):
    beta = -combine(part_ref[...]) - log_a
    pot_ref[...] = (beta + b2_ref[...]) * (eps / LOG2E)
    bwide_ref[...] = jnp.broadcast_to(beta + log_b, bwide_ref.shape)


def turn_sum_kernel(order, *refs):
    parts, outs = refs[:2], refs[2:]
    n = outs[0].shape[0]
    for out_ref, first in zip(outs, order()):
        rows = pl.ds(pl.multiple_of(first * n, n), n)
        out_ref[...] = tree(jnp.add, [part[rows, :] for part in parts])


def sum_kernel(*refs):
    refs[-1][...] = tree(jnp.add, [part[...] for part in refs[:-1]])


VM = pl.BlockSpec(memory_space=pltpu.VMEM)


def call(kernel, outs, scratch, *args, limit=6 * MIB, cost=None, ins=None):
    return pl.pallas_call(
        kernel,
        out_shape=outs,
        in_specs=ins or [VM] * len(args),
        out_specs=[VM] * len(outs),
        scratch_shapes=scratch,
        cost_estimate=cost,
        compiler_params=pltpu.CompilerParams(vmem_limit_bytes=limit),
    )(*args)


def f32(*shape):
    return jax.ShapeDtypeStruct(shape, jnp.float32)


def v16(*shape):
    return pltpu.VMEM(shape, jnp.bfloat16)


def v32(*shape):
    return pltpu.VMEM(shape, jnp.float32)


def spread(x, axis):
    return lax.all_to_all(x, axis, 0, 0, tiled=True)


def body(points_a, points_b):
    na, nb = lax.axis_size("aa"), lax.axis_size("ba")
    share, width = points_a.shape
    piece = points_b.shape[0]
    rows_a, rows_b = share * nb, piece * na
    eps = width / 8.0
    log_a = -math.log2(rows_a * na)
    log_b = -math.log2(rows_b * nb)

    def move(x, by):
        return lax.ppermute(x, "aa", [(i, (i + 2 * by) % na) for i in range(na)])

    def swap(x):
        return lax.ppermute(x, "aa", [(i, i ^ 1) for i in range(na)])

    def place(by, flip, start=0):
        return lambda me: lax.rem(lax.bitwise_xor(me, flip) + 2 * by, na) * piece + start

    half = piece // 2
    up, down = move(points_b, 1), move(points_b, -1)
    low, high = move(up[:half], 1), move(down[half:], -1)
    wide, = call(repeat_kernel, [v32(nb, share, width)], [], points_a)
    whole_a = spread(wide, "ba").reshape(rows_a, width)
    pieces = [
        (points_b, place(0, 0)), (up, place(3, 0)), (down, place(1, 0)), (low, place(2, 0)), (high, place(2, 0, half)),
        (swap(points_b), place(0, 1)), (swap(up), place(3, 1)), (swap(down), place(1, 1)),
        (swap(low), place(2, 1)), (swap(high), place(2, 1, half))]
    left, a2, bhi, blo, b2 = call(
        lambda *r: pieces_kernel(eps, [p for x, p in pieces], *r),
        [v16(rows_a, 3 * width), v32(1, rows_a), v16(rows_b, width), v16(rows_b, width), v32(1, rows_b)],
        [v32(rows_b, width), pltpu.SemaphoreType.DMA((len(pieces),))],
        whole_a, *[x for x, p in pieces], limit=12 * MIB,
        ins=[VM] + [pl.BlockSpec(memory_space=pl.ANY)] * len(pieces))
    s, rows = call(
        lambda *r: scores_kernel(piece, *r),
        [v32(rows_a, rows_b), v32(nb, rows_a)], [v32(rows_a, LANES), v32(rows_a, LANES)],
        left, bhi, blo, b2, limit=8 * MIB)
    for turn in range(ITERS):
        if turn > 0:
            rows, = call(
                lambda *r: row_pass_kernel(log_a, *r),
                [f32(nb, rows_a)],
                [v32(8, rows_b), v32(rows_a, LANES), v32(rows_a, LANES)],
                part, s)
        final = turn == ITERS - 1
        wide_shape = [v32(rows_a, LANES)]
        cols, pot_a, *awide = call(
            lambda *r: col_pass_kernel(log_b, eps, *r),
            [f32(na, rows_b), f32(1, rows_a)] + wide_shape * final, wide_shape * (not final),
            spread(rows, "ba"), a2, s)
        part = spread(cols, "aa")
    def along_x(v, by):
        return lax.ppermute(v, "ba", [(i, (i + side * by) % nb) for i in range(nb)])

    def along_y(v, by):
        return lax.ppermute(v, "ba", [(i, i // side * side + (i + by) % side) for i in range(nb)])

    side = math.isqrt(nb)
    step = pl.CostEstimate(flops=2 * rows_a // side * width * rows_b, bytes_accessed=MIB, transcendentals=0)
    held = []
    bwide, pot_b = call(
        lambda *r: weights_kernel(log_a, log_b, eps, *r), [v32(8, rows_b), f32(1, rows_b)], [], part, b2)
    for by in [2, 1, 3, 0]:
        g, = call(
            lambda *r: grad_kernel(lambda: lax.rem(lax.axis_index("ba") // side + by, side) * (rows_a // side), *r),
            [v32(rows_a // side, width)], [v32(rows_a // side, LANES)],
            *awide, bwide, whole_a, bhi, blo, s, limit=12 * MIB, cost=step)
        held.append(along_x(g, by) if by else g)
    *arrived, total = held
    long = pl.CostEstimate(flops=9 * step.flops, bytes_accessed=4 * MIB, transcendentals=0)
    for g in arrived[:-1]:
        total, = call(sum_kernel, [v32(rows_a // side, width)], [], total, g, cost=long)
    cuts = call(
        lambda *r: turn_sum_kernel(lambda: [lax.rem(lax.rem(lax.axis_index("ba"), side) + by, side) for by in range(side)], *r),
        [v32(share, width)] * side, [], total, arrived[-1])
    grad, = call(sum_kernel, [f32(share, width)], [], cuts[0], *[along_y(cuts[by], by) for by in (2, 1, 3)])
    return (pot_a.reshape(rows_a), pot_b.reshape(rows_b), grad)


def solution(mesh):
    placed = (P(("aa", "ba"), None), P(("ba", "aa"), None))
    return jax.shard_map(
        body,
        mesh=mesh,
        in_specs=placed,
        out_specs=(P("aa"), P("ba"), P(("aa", "ba"), None)),
        check_vma=False,
    )
```
